128 devices in a mesh: row: 16 (over x_lo, z, core), col: 8 (over x_hi, y).
Axes of the slice: x: 4 (x_hi: 2, x_lo: 2; x = x_hi * 2 + x_lo), y: 4, z: 4, core: 2. Of those that a mesh axis runs over, the one named last changes fastest.
Arguments:
- u_start: float32 [128, 262144], P('col', 'row'), may hold values from -24 to 24
- v_start: float32 [128, 131072], P('row', 'col'), may hold values from -24 to 24
- keep_u: float32 [128, 40], replicated, may hold values from -1 to 1, as said below
- keep_v: float32 [128, 40], replicated, may hold values from -1 to 1, as said below
- v_next: float32 [131072], P(('col', 'row')), may hold values from -96 to 96
- tile_blocks: bfloat16 [8192, 256, 256], P(('row', 'col')), may hold values from -0.375 to 0.375
- tile_rows: int32 [8192], P(('row', 'col')), may hold values from 0 to 63
- tile_cols: int32 [8192], P(('row', 'col')), may hold values from 0 to 63
- tile_count: int32 [128], P(('row', 'col')), may hold values from 32 to 64
Outputs:
- u_basis: float32 [42, 262144], P(None, ('row', 'col'))
- v_basis: float32 [43, 131072], P(None, ('col', 'row'))
- bidiagonal: float32 [2, 2], replicated
The draws below stay inside these ranges and needn't reach their ends.
Inputs may be any that keep to these rules, and one draw needn't show every extreme that they name: `tile_rows`: tile row within the device's row group. `tile_cols`: tile column within the device's column group. `tile_count`: slots at this index and beyond hold no tile. `keep_u`: the columns are orthonormal. `keep_v`: the columns are orthonormal.
All inputs are finite; a program needn't handle non-finite values.
Results may differ from the reference program's by a relative error of at most 0.00155.
Values may be sent and summed in bfloat16 or wider, within the bound.
No kernel may reach another device: no remote copies, remote signals or barrier semaphores. Data moves between devices by JAX's collectives and lax.ppermute only.
A program may use at most 64 MiB of HBM per device.

```python
import jax
import jax.numpy as jnp
from jax import lax

BASIS = 128
KEEP = 40
TILE = 256
STEPS = 2
RB = 64
CB = 64
TILES_DEV = 64
M = 262144
N = 131072
TILES = 8192
N_COL = 8
DEVICES = 128


def basis_rows_draw(key, count, length):
    raw = jax.random.normal(jax.random.fold_in(key, 1), (length, count), jnp.float32)
    factor, upper = jnp.linalg.qr(raw)
    rows = factor.T * jnp.sqrt(jnp.float32(length))
    along = jnp.arange(length, dtype=jnp.float32) / jnp.float32(length)
    inner = along * jnp.float32(N_COL) - jnp.floor(along * jnp.float32(N_COL))
    weight = (1.0 + 2.0 * along) * (1.0 + 2.0 * inner)
    row_scale = jax.random.uniform(jax.random.fold_in(key, 2), (count, 1), jnp.float32, 0.7, 1.3)
    rows = rows * weight[None, :]
    rows = rows / jnp.sqrt(jnp.mean(rows * rows, axis=1, keepdims=True))
    rows = rows * row_scale
    return jnp.clip(rows, -24.0, 24.0).astype(jnp.float32)


def columns_draw(key, count, width):
    raw = jax.random.normal(key, (count, width), jnp.float32)
    factor, upper = jnp.linalg.qr(raw)
    return factor.astype(jnp.float32)


def draw_u_start(key, part):
    return basis_rows_draw(jax.random.fold_in(key, 11), BASIS, M)


def draw_v_start(key, part):
    return basis_rows_draw(jax.random.fold_in(key, 23), BASIS, N)


def draw_keep_u(key, part):
    return columns_draw(jax.random.fold_in(key, 37), BASIS, KEEP)


def draw_keep_v(key, part):
    return columns_draw(jax.random.fold_in(key, 41), BASIS, KEEP)


def draw_v_next(key, part):
    rows = basis_rows_draw(jax.random.fold_in(key, 23), BASIS, N)
    mixing = 0.5 * jax.random.normal(jax.random.fold_in(key, 59), (BASIS,), jnp.float32)
    noise = jax.random.normal(jax.random.fold_in(key, 61), (N,), jnp.float32)
    mixed = noise + jnp.dot(mixing, rows, precision=jax.lax.Precision.HIGHEST)
    return jnp.clip(mixed, -96.0, 96.0).astype(jnp.float32)


def plant(entries, stream_key, low, high):
    spot = [jax.random.randint(jax.random.fold_in(stream_key, axis), (), 0, length) for axis, length in enumerate(entries.shape)]
    longest = entries.shape.index(max(entries.shape))
    neighbour = spot[:longest] + [(spot[longest] + 1) % entries.shape[longest]] + spot[longest + 1:]
    return entries.at[tuple(spot)].set(low).at[tuple(neighbour)].set(high)


def level_of(own_key, extent, pieces, low, largest):
    def one(position, blocks):
        heights = jax.random.uniform(jax.random.fold_in(jax.random.fold_in(own_key, 6), position), (blocks,), jnp.float32, low / len(pieces), largest / len(pieces))
        return jnp.repeat(jnp.exp(heights), extent[position] // blocks).reshape((-1,) + (1,) * (len(extent) - position - 1))

    level = one(*pieces[0])
    for cut in pieces[1:]:
        level = level * one(*cut)
    return level


def scatter_about(rng, shape, deviation, limit, shards=(), kind=jnp.bfloat16):
    gain = level_of(rng, shape, shards, -0.22, 0.18) if shards else 1.0
    array = jax.random.normal(rng, shape, jnp.float32) * deviation * gain
    return jnp.minimum(jnp.maximum(array, -limit), limit).astype(kind)


def setup_inputs(seed: int = 0) -> dict:
    splits = jax.random.split(jax.random.key(seed), 10)
    u_start = draw_u_start(jax.random.fold_in(splits[9], 71), 0)
    v_start = draw_v_start(jax.random.fold_in(splits[9], 71), 0)
    keep_u = draw_keep_u(jax.random.fold_in(splits[9], 71), 0)
    keep_v = draw_keep_v(jax.random.fold_in(splits[9], 71), 0)
    v_next = draw_v_next(jax.random.fold_in(splits[9], 71), 0)
    tile_blocks = scatter_about(splits[5], (TILES, TILE, TILE), TILE ** -0.5, 0.375, ((0, 128),))
    tile_rows = plant(jax.random.randint(splits[6], (TILES,), 0, RB), jax.random.fold_in(splits[6], 1), 0, RB - 1).astype(jnp.int32)
    tile_cols = plant(jax.random.randint(splits[7], (TILES,), 0, CB), jax.random.fold_in(splits[7], 1), 0, CB - 1).astype(jnp.int32)
    tile_count = plant(jax.random.randint(splits[8], (DEVICES,), TILES_DEV // 2, TILES_DEV + 1), jax.random.fold_in(splits[8], 1), TILES_DEV // 2, TILES_DEV).astype(jnp.int32)
    return {"u_start": u_start, "v_start": v_start, "keep_u": keep_u, "keep_v": keep_v, "v_next": v_next, "tile_blocks": tile_blocks, "tile_rows": tile_rows, "tile_cols": tile_cols, "tile_count": tile_count}


HIGH = lax.Precision.HIGHEST

def tile_product(tile_blocks, tile_rows, tile_cols, tile_count, vector, forward_pass):
    rounded = lax.optimization_barrier(vector.astype(jnp.bfloat16)).astype(jnp.float32)
    if forward_pass:
        blocks = rounded.reshape(N // TILE, TILE)
        segments = M // TILE
    else:
        blocks = rounded.reshape(M // TILE, TILE)
        segments = N // TILE
    grouped = tile_blocks.reshape(DEVICES, TILES_DEV, TILE, TILE)
    row_slots = tile_rows.reshape(DEVICES, TILES_DEV)
    col_slots = tile_cols.reshape(DEVICES, TILES_DEV)

    def per_device(device):
        row_group = device // N_COL
        col_group = device % N_COL
        tile_float = lax.dynamic_index_in_dim(grouped, device, 0, keepdims=False).astype(jnp.float32)
        local_rows = lax.dynamic_index_in_dim(row_slots, device, 0, keepdims=False)
        local_cols = lax.dynamic_index_in_dim(col_slots, device, 0, keepdims=False)
        active = (jnp.arange(TILES_DEV, dtype=jnp.int32) < tile_count[device]).astype(jnp.float32)
        row_index = (row_group * RB + local_rows).astype(jnp.int32)
        col_index = (col_group * CB + local_cols).astype(jnp.int32)
        if forward_pass:
            picked = blocks[col_index]
            outputs = jnp.einsum('tij,tj->ti', tile_float, picked, precision=HIGH)
            target = row_index
        else:
            picked = blocks[row_index]
            outputs = jnp.einsum('tij,ti->tj', tile_float, picked, precision=HIGH)
            target = col_index
        return (outputs * active[:, None], target)
    outputs, target = lax.map(per_device, jnp.arange(DEVICES, dtype=jnp.int32))
    summed = jax.ops.segment_sum(outputs.reshape(-1, TILE), target.reshape(-1), num_segments=segments)
    return summed.reshape(-1)

def orthonormal(basis_rows, vector):
    length = vector.shape[0]
    first_coef = jnp.dot(basis_rows, vector, precision=HIGH) / length
    once_clean = vector - jnp.dot(first_coef, basis_rows, precision=HIGH)
    second_coef = jnp.dot(basis_rows, once_clean, precision=HIGH) / length
    twice_clean = once_clean - jnp.dot(second_coef, basis_rows, precision=HIGH)
    scale_now = jnp.sqrt(jnp.sum(twice_clean * twice_clean) / length + 1e-06)
    return (twice_clean / scale_now, scale_now)

def reference(u_start, v_start, keep_u, keep_v, v_next, tile_blocks, tile_rows, tile_cols, tile_count):
    u_kept = jnp.dot(keep_u.T, u_start, precision=HIGH)
    v_kept = jnp.dot(keep_v.T, v_start, precision=HIGH)
    first_right, beta_start = orthonormal(v_kept, v_next)
    left_rows = u_kept
    right_rows = jnp.concatenate([v_kept, first_right[None, :]], axis=0)
    current = first_right
    alpha_list = []
    beta_list = []
    for iteration in range(STEPS):
        image = tile_product(tile_blocks, tile_rows, tile_cols, tile_count, current, True)
        left_new, alpha = orthonormal(left_rows, image)
        left_rows = jnp.concatenate([left_rows, left_new[None, :]], axis=0)
        back_image = tile_product(tile_blocks, tile_rows, tile_cols, tile_count, left_new, False)
        current, beta = orthonormal(right_rows, back_image)
        right_rows = jnp.concatenate([right_rows, current[None, :]], axis=0)
        alpha_list.append(alpha)
        beta_list.append(beta)
    bidiagonal = jnp.stack([jnp.stack(alpha_list), jnp.stack(beta_list)])
    return (left_rows, right_rows, bidiagonal)
```

```python
import jax
import jax.numpy as jnp
from jax import lax
from jax.sharding import Mesh
from jax.sharding import PartitionSpec as P

STEPS = 2
ROW = ("row_0", "row_1", "row_2")
COL = ("col_0", "col_1")
ROW_COL = ROW + COL
COL_ROW = COL + ROW

HIGH = lax.Precision.HIGHEST


def swapped(blocks, axis):
    return lax.all_to_all(blocks, axis, 0, 0, tiled=True)


def in_blocks(x, devices):
    rows, length = x.shape
    return jnp.moveaxis(x.reshape(rows, devices, length // devices), 1, 0)


def from_everyone(x, axis):
    return swapped(jnp.broadcast_to(x[None], (lax.axis_size(axis), *x.shape)), axis)


def summed_everywhere(x):
    return jnp.sum(from_everyone(x, ROW_COL), axis=0)


def kept(start, keep, axis):
    here = swapped(in_blocks(start, lax.axis_size(axis)), axis)
    return jnp.dot(keep.T, here.reshape(-1, here.shape[-1]), precision=HIGH)


def orthonormal(basis, vector, gram, dots, square):
    coef = 2.0 * dots - jnp.dot(gram, dots, precision=HIGH)
    clean = vector - jnp.dot(coef, basis, precision=HIGH)
    across = dots - jnp.dot(gram, coef, precision=HIGH)
    mean_square = square - jnp.dot(coef, dots, precision=HIGH) - jnp.dot(coef, across, precision=HIGH)
    scale = jnp.sqrt(jnp.maximum(mean_square, 0.0) + 1e-06)
    new = clean / scale
    across = across / scale
    own = mean_square / (scale * scale)
    grown = jnp.concatenate(
        [
            jnp.concatenate([gram, across[:, None]], axis=1),
            jnp.concatenate([across, own[None]])[None, :],
        ],
        axis=0,
    )
    return new, scale, grown


def per_device(
    u_start, v_start, keep_u, keep_v, v_next, tile_blocks, tile_rows, tile_cols, tile_count
):
    total = lax.axis_size(ROW_COL)
    v_kept = kept(v_start, keep_v, ROW)
    u_kept = kept(u_start, keep_u, COL)
    u_length = u_kept.shape[1] * total
    v_length = v_kept.shape[1] * total
    slots, size = tile_blocks.shape[:2]
    row_blocks = u_kept.shape[1] * lax.axis_size(COL) // size
    col_blocks = v_kept.shape[1] * lax.axis_size(ROW) // size
    active = jnp.arange(slots, dtype=jnp.int32) < tile_count[0]
    row_hot = (
        (tile_rows[None, :] == jnp.arange(row_blocks, dtype=jnp.int32)[:, None]) & active[None, :]
    ).astype(jnp.float32)
    col_hot = (
        (tile_cols[None, :] == jnp.arange(col_blocks, dtype=jnp.int32)[:, None]) & active[None, :]
    ).astype(jnp.float32)

    keep_count = v_kept.shape[0]
    stacked = jnp.concatenate([v_kept, v_next[None, :]], axis=0)
    first = summed_everywhere(
        jnp.dot(stacked, stacked.T, precision=HIGH).reshape(-1)
    ).reshape(keep_count + 1, keep_count + 1) / v_length
    current, _, gram_v = orthonormal(
        v_kept, v_next, first[:keep_count, :keep_count], first[keep_count, :keep_count], first[keep_count, keep_count]
    )
    right = jnp.concatenate([v_kept, current[None, :]], axis=0)
    left = u_kept
    gram_u = None
    alphas = []
    betas = []
    for step in range(STEPS):
        wide = from_everyone(current.astype(jnp.bfloat16), ROW).reshape(col_blocks, size)
        products = jnp.einsum(
            "tij,tj->ti", tile_blocks, wide[tile_cols], preferred_element_type=jnp.float32
        )
        partial = jnp.dot(row_hot, products, precision=HIGH)
        image = jnp.sum(swapped(partial.reshape(lax.axis_size(COL), -1), COL), axis=0)
        if gram_u is None:
            stacked = jnp.concatenate([left, image[None, :]], axis=0)
            first = summed_everywhere(
                jnp.dot(stacked, stacked.T, precision=HIGH).reshape(-1)
            ).reshape(keep_count + 1, keep_count + 1) / u_length
            gram_u, dots, square = first[:keep_count, :keep_count], first[keep_count, :keep_count], first[keep_count, keep_count]
        else:
            stacked = jnp.concatenate([left, image[None, :]], axis=0)
            first = summed_everywhere(jnp.dot(stacked, image, precision=HIGH)) / u_length
            dots, square = first[:-1], first[-1]
        new, alpha, gram_u = orthonormal(left, image, gram_u, dots, square)
        left = jnp.concatenate([left, new[None, :]], axis=0)
        wide = from_everyone(new.astype(jnp.bfloat16), COL).reshape(row_blocks, size)
        products = jnp.einsum(
            "tij,ti->tj", tile_blocks, wide[tile_rows], preferred_element_type=jnp.float32
        )
        partial = jnp.dot(col_hot, products, precision=HIGH)
        image = jnp.sum(swapped(partial.reshape(lax.axis_size(ROW), -1), ROW), axis=0)
        stacked = jnp.concatenate([right, image[None, :]], axis=0)
        first = summed_everywhere(jnp.dot(stacked, image, precision=HIGH)) / v_length
        current, beta, gram_v = orthonormal(right, image, gram_v, first[:-1], first[-1])
        right = jnp.concatenate([right, current[None, :]], axis=0)
        alphas.append(alpha)
        betas.append(beta)
    return left, right, jnp.stack([jnp.stack(alphas), jnp.stack(betas)])


def solution(mesh):
    finer = Mesh(mesh.devices.reshape(2, 4, 2, 2, 4), ROW_COL)
    return jax.shard_map(
        per_device,
        mesh=finer,
        in_specs=(
            P(COL, ROW),
            P(ROW, COL),
            P(),
            P(),
            P(COL_ROW),
            P(ROW_COL, None, None),
            P(ROW_COL),
            P(ROW_COL),
            P(ROW_COL),
        ),
        out_specs=(P(None, ROW_COL), P(None, COL_ROW), P()),
        check_vma=False,
    )
```

```python
import functools

import jax
import jax.numpy as jnp
from jax import lax
from jax.experimental import pallas as pl
from jax.experimental.pallas import tpu as pltpu
from jax.sharding import Mesh
from jax.sharding import PartitionSpec as P

ROW = ("row_0", "row_1", "row_2")
COL = ("col_0", "col_1")
ROW_COL = ROW + COL
COL_ROW = COL + ROW

HIGH = lax.Precision.HIGHEST
F32 = jnp.float32
BF16 = jnp.bfloat16
LANES = 128
PAD = 48
EPS = 1e-06
VMEM_LIMIT = 30 << 20


def swapped(blocks, axis):
    return lax.all_to_all(blocks, axis, 0, 0, tiled=True)


def iota(shape, dim):
    return lax.broadcasted_iota(jnp.int32, shape, dim)


def as_row(col):
    spot = iota((PAD, LANES), 0) == iota((PAD, LANES), 1)
    return jnp.sum(jnp.where(spot, col, 0.0), axis=0, keepdims=True)


def as_col(row):
    spot = iota((PAD, LANES), 0) == iota((PAD, LANES), 1)
    return jnp.sum(jnp.where(spot, row, 0.0), axis=1, keepdims=True)


def total(x):
    return jnp.sum(jnp.sum(x, axis=1, keepdims=True), axis=0, keepdims=True)


def packed(gram, n):
    width = n // 2 + 1
    twice = gram + pltpu.roll(gram, n, 1)
    turned, sub = twice, iota((PAD, LANES), 0)
    for bit in (1, 2, 4, 8, 16, 32):
        turned = jnp.where(sub & bit != 0, pltpu.roll(turned, LANES - bit, 1), turned)
    turned = jnp.where(iota((PAD, LANES), 1) < width, turned, 0.0)
    out = turned[0:8]
    for g in range(1, PAD // 8):
        out = out + pltpu.roll(turned[8 * g : 8 * g + 8], width * g, 1)
    return out


def unpacked(pack, n):
    width = n // 2 + 1
    groups = [pack] + [
        pltpu.roll(pack, LANES - width * g, 1) for g in range(1, PAD // 8)
    ]
    turned = jnp.concatenate(groups, axis=0)
    turned = jnp.where(iota((PAD, LANES), 1) < width, turned, 0.0)
    wide = pltpu.roll(turned, 0, 1, stride=1, stride_axis=0)
    half = wide + pltpu.roll(wide, LANES - n, 1)
    lane, sub = iota((PAD, LANES), 1), iota((PAD, LANES), 0)
    half = jnp.where((lane < n) & (sub < n), half, 0.0)
    square = jnp.concatenate([half, jnp.zeros((LANES - PAD, LANES), F32)], axis=0)
    return half + jnp.where(lane == sub, 0.0, square.T[:PAD])


def solve(gram, dots_col, square, m):
    coef_col = 2.0 * dots_col - jnp.sum(gram * as_row(dots_col), axis=1, keepdims=True)
    across = dots_col - jnp.sum(gram * as_row(coef_col), axis=1, keepdims=True)
    mean_square = square - total(coef_col * (dots_col + across))
    mean_square = jnp.maximum(mean_square, 0.0)
    scale = jnp.sqrt(mean_square + EPS)
    inverse = 1.0 / scale
    across = across * inverse
    lane, sub = iota((PAD, LANES), 1), iota((PAD, LANES), 0)
    grown = jnp.where(sub == m, as_row(across), gram)
    grown = jnp.where(lane == m, across, grown)
    grown = jnp.where((lane == m) & (sub == m), mean_square * inverse * inverse, grown)
    return coef_col, scale, inverse, grown


def at(value, index):
    return jnp.where(iota((PAD, 1), 0) == index, value, 0.0)


def padded(col):
    return jnp.concatenate([col, jnp.zeros((PAD - col.shape[0], 1), F32)], axis=0)


def regroup_kernel(start_ref, out_ref):
    out_ref[...] = start_ref[...][None]


def kept_kernel(start_ref, keep_ref, out_ref, gram_ref):
    basis = lax.dot_general(
        keep_ref[...], start_ref[...], (((0,), (0,)), ((), ())), precision=HIGH, preferred_element_type=F32
    )
    out_ref[...] = basis
    rows = basis.shape[0]
    wide = jnp.concatenate([basis, jnp.zeros((PAD - rows, basis.shape[1]), F32)], axis=0)
    full = jnp.concatenate([wide, jnp.zeros((LANES - PAD, basis.shape[1]), F32)], axis=0)
    gram = lax.dot_general(
        wide, full, (((1,), (1,)), ((), ())), precision=HIGH, preferred_element_type=F32
    )
    gram_ref[...] = packed(gram, rows + 1)


def kept_with_kernel(start_ref, keep_ref, next_ref, out_ref, message_ref, wide_ref):
    basis = lax.dot_general(
        keep_ref[...], start_ref[...], (((0,), (0,)), ((), ())), precision=HIGH, preferred_element_type=F32
    )
    out_ref[...] = basis
    rows = basis.shape[0]
    wide_ref[...] = jnp.zeros_like(wide_ref)
    wide_ref[:rows] = basis
    for j in range(next_ref.shape[0]):
        wide_ref[rows : rows + 1, j * LANES : (j + 1) * LANES] = next_ref[j : j + 1]
    full = wide_ref[...]
    gram = lax.dot_general(
        full[:PAD], full, (((1,), (1,)), ((), ())), precision=HIGH, preferred_element_type=F32
    )
    message_ref[...] = jnp.broadcast_to(packed(gram, rows + 1)[None], message_ref.shape)


def projected_slice(vector_ref, basis_ref, coef_col):
    count = basis_ref.shape[0]
    rows = []
    for j in range(vector_ref.shape[0]):
        part = basis_ref[:, j * LANES : (j + 1) * LANES] * coef_col[:count]
        rows.append(jnp.sum(part, axis=0, keepdims=True))
    return vector_ref[...] - jnp.concatenate(rows, axis=0)


def first_kernel(length, got_ref, basis_ref, next_ref, vector_ref, gram_ref, message_ref):
    count = basis_ref.shape[0]
    gram = unpacked(jnp.sum(got_ref[...], axis=0), count + 1) * (1.0 / length)
    lane, sub = iota((PAD, LANES), 1), iota((PAD, LANES), 0)
    dots = jnp.sum(jnp.where((lane == count) & (sub < count), gram, 0.0), axis=1, keepdims=True)
    square = total(jnp.where((lane == count) & (sub == count), gram, 0.0))
    gram = jnp.where((lane < count) & (sub < count), gram, 0.0)
    coef, scale, inverse, grown = solve(gram, dots, square, count)
    new = projected_slice(next_ref, basis_ref, coef) * inverse
    vector_ref[...] = new
    gram_ref[...] = grown
    message_ref[...] = jnp.broadcast_to(new[None], message_ref.shape)


def multiplied(forward, entries, tiles_ref, pick_ref, place_ref, count_ref, picked_ref, product_ref):
    slots, size = tiles_ref.shape[:2]
    blocks = size // LANES
    rows = entries.shape[0]
    values = entries.astype(BF16)
    lane = iota((slots, rows), 1)
    for b in range(blocks):
        hot = (lane == blocks * pick_ref[...] + b).astype(BF16)
        picked_ref[:, b * LANES : (b + 1) * LANES] = jnp.dot(hot, values, preferred_element_type=F32)
    for t in range(slots):
        product_ref[t : t + 1] = lax.dot_general(
            picked_ref[t : t + 1].astype(BF16),
            tiles_ref[t],
            (((1,), (1 if forward else 0,)), ((), ())),
            preferred_element_type=F32,
        )
    sub, slot = iota((rows, slots), 0), iota((rows, slots), 1)
    out = None
    for b in range(blocks):
        hot = ((sub == blocks * place_ref[...] + b) & (slot < count_ref[0])).astype(F32)
        part = jnp.dot(
            hot, product_ref[:, b * LANES : (b + 1) * LANES], precision=HIGH, preferred_element_type=F32
        )
        out = part if out is None else out + part
    return out


def forward_kernel(
    extra, got_ref, tiles_ref, pick_ref, place_ref, count_ref, *refs
):
    if extra:
        gram_ref, message_ref, picked_ref, product_ref = refs
    else:
        message_ref, picked_ref, product_ref = refs
    entries = got_ref[...].reshape(-1, LANES)
    sums = multiplied(True, entries, tiles_ref, pick_ref, place_ref, count_ref, picked_ref, product_ref)
    rows = sums.shape[0]
    for k in range(message_ref.shape[0]):
        message_ref[k, :rows] = sums
        if extra:
            message_ref[k, rows:] = gram_ref[...]


def left_dots_kernel(length, got_ref, wide_ref, *refs):
    refs = list(refs)
    first = got_ref.shape[1] > LANES
    others = [] if first else [refs.pop(0)]
    image_ref, message_ref = refs
    image = jnp.sum(got_ref[:, :LANES], axis=0)
    image_ref[...] = image
    parts, count, width = wide_ref.shape
    across = width // LANES
    acc = jnp.zeros((count, LANES), F32)
    for k in range(parts):
        for j in range(across):
            r = k * across + j
            acc = acc + wide_ref[k, :, j * LANES : (j + 1) * LANES] * image_ref[r : r + 1]
    dots = padded(jnp.sum(acc, axis=1, keepdims=True))
    for n, other in enumerate(others):
        dots = dots + at(total(other[...] * image), count + n)
    dots = dots + at(total(image * image), PAD - 1)
    row = as_row(dots) * (1.0 / length)
    if first:
        gram = jnp.sum(got_ref[:, LANES:], axis=0) * (1.0 / length)
        message_ref[:, :8] = jnp.broadcast_to(gram[None], (message_ref.shape[0], 8, LANES))
        message_ref[:, 8:] = jnp.broadcast_to(row[None], (message_ref.shape[0], 8, LANES))
    else:
        message_ref[...] = jnp.broadcast_to(row, message_ref.shape)


def split_dots(row):
    col = as_col(row)
    last = iota((PAD, 1), 0) == PAD - 1
    return jnp.where(last, 0.0, col), total(jnp.where(last, col, 0.0))


def left_kernel(
    m, got_ref, image_ref, wide_ref, tiles_ref, pick_ref, place_ref, count_ref, own_ref, *refs
):
    refs = list(refs)
    first = len(got_ref.shape) == 3
    gram_in = None if first else refs.pop(0)
    others = [] if first else [refs.pop(0)]
    new_ref, own_out_ref, gram_ref, scale_ref, message_ref, picked_ref, product_ref = refs
    parts, count, width = wide_ref.shape
    if first:
        got = jnp.sum(got_ref[...], axis=0)
        gram = unpacked(got[:8], count + 1)
        row = got[8:9]
    else:
        gram = gram_in[...]
        row = jnp.sum(got_ref[...], axis=0, keepdims=True)
    dots, square = split_dots(row)
    coef, scale, inverse, grown = solve(gram, dots, square, m)
    gram_ref[...] = grown
    scale_ref[...] = jnp.broadcast_to(scale, scale_ref.shape)
    across = width // LANES
    by_lane = jnp.broadcast_to(coef[:count], (count, LANES))
    for k in range(parts):
        for j in range(across):
            r = k * across + j
            part = wide_ref[k, :, j * LANES : (j + 1) * LANES] * by_lane
            new_ref[r : r + 1] = image_ref[r : r + 1] - jnp.sum(part, axis=0, keepdims=True)
    new = new_ref[...]
    for n, other in enumerate(others):
        new = new - coef[count + n : count + n + 1] * other[...]
    new = new * inverse
    new_ref[...] = new
    own_out_ref[...] = new_ref[pl.ds(pl.multiple_of(own_ref[0] * across, across), across)]
    sums = multiplied(False, new, tiles_ref, pick_ref, place_ref, count_ref, picked_ref, product_ref)
    message_ref[...] = sums.reshape(message_ref.shape)


def right_dots_kernel(length, got_ref, basis_ref, *refs):
    refs = list(refs)
    image_ref, message_ref = refs[-2:]
    others = refs[:-2]
    image = jnp.sum(got_ref[...], axis=0)
    image_ref[...] = image
    count = basis_ref.shape[0]
    acc = jnp.zeros((count, LANES), F32)
    for j in range(image.shape[0]):
        acc = acc + basis_ref[:, j * LANES : (j + 1) * LANES] * image_ref[j : j + 1]
    dots = padded(jnp.sum(acc, axis=1, keepdims=True))
    for n, other in enumerate(others):
        dots = dots + at(total(other[...] * image), count + n)
    dots = dots + at(total(image * image), PAD - 1)
    message_ref[...] = jnp.broadcast_to(as_row(dots) * (1.0 / length), message_ref.shape)


def new_right(m, got_ref, image_ref, basis_ref, gram_ref, others):
    count = basis_ref.shape[0]
    dots, square = split_dots(jnp.sum(got_ref[...], axis=0, keepdims=True))
    coef, scale, inverse, grown = solve(gram_ref[...], dots, square, m)
    new = projected_slice(image_ref, basis_ref, coef)
    for n, other in enumerate(others):
        new = new - coef[count + n : count + n + 1] * other[...]
    return new * inverse, scale, grown


def right_kernel(m, got_ref, image_ref, basis_ref, gram_in_ref, *refs):
    refs = list(refs)
    vector_ref, gram_ref, scale_ref, message_ref = refs[-4:]
    new, scale, grown = new_right(m, got_ref, image_ref, basis_ref, gram_in_ref, refs[:-4])
    vector_ref[...] = new
    gram_ref[...] = grown
    scale_ref[...] = jnp.broadcast_to(scale, scale_ref.shape)
    message_ref[...] = jnp.broadcast_to(new[None], message_ref.shape)


def put_rows(out_ref, row, vector):
    for j in range(vector.shape[0]):
        out_ref[row : row + 1, j * LANES : (j + 1) * LANES] = vector[j : j + 1]


def last_kernel(
    m, got_ref, image_ref, basis_ref, gram_ref, old_0_ref, old_1_ref,
    alpha_0_ref, alpha_1_ref, beta_0_ref, out_ref, scales_ref,
):
    new, scale, _ = new_right(m, got_ref, image_ref, basis_ref, gram_ref, [old_0_ref, old_1_ref])
    count = basis_ref.shape[0]
    out_ref[:count] = basis_ref[...]
    put_rows(out_ref, count, old_0_ref[...])
    put_rows(out_ref, count + 1, old_1_ref[...])
    put_rows(out_ref, count + 2, new)
    lane = iota((1, LANES), 1)
    alphas = jnp.where(lane == 0, alpha_0_ref[...], alpha_1_ref[...])
    betas = jnp.where(lane == 0, beta_0_ref[...], jnp.broadcast_to(scale, (1, LANES)))
    scales_ref[...] = jnp.concatenate([alphas, betas], axis=0)[:, :2]


def left_out_kernel(basis_ref, new_0_ref, new_1_ref, out_ref):
    count = basis_ref.shape[0]
    out_ref[:count] = basis_ref[...]
    put_rows(out_ref, count, new_0_ref[...])
    put_rows(out_ref, count + 1, new_1_ref[...])


WHOLE = pl.BlockSpec(memory_space=pltpu.VMEM)
SCALAR = pl.BlockSpec(memory_space=pltpu.SMEM)


def call(kernel, name, outs, args, scalars=(), scratch=()):
    shapes = tuple(jax.ShapeDtypeStruct(s, F32) for s in outs)
    result = pl.pallas_call(
        kernel,
        name=name,
        out_shape=shapes,
        in_specs=[SCALAR if i in scalars else WHOLE for i in range(len(args))],
        out_specs=tuple(WHOLE for _ in shapes),
        scratch_shapes=list(scratch),
        compiler_params=pltpu.CompilerParams(vmem_limit_bytes=VMEM_LIMIT),
    )(*args)
    return result


def per_device(
    u_start, v_start, keep_u, keep_v, v_next, tile_blocks, tile_rows, tile_cols, tile_count
):
    rows_n, cols_n = lax.axis_size(ROW), lax.axis_size(COL)
    devices = rows_n * cols_n
    keep = keep_u.shape[1]
    slots, size = tile_blocks.shape[:2]
    u_here, u_range = u_start.shape
    v_here, v_range = v_start.shape
    u_own, v_own = u_range // cols_n, v_range // rows_n
    u_length, v_length = u_range * rows_n, v_range * cols_n
    u_rows, v_rows = u_own // LANES, v_own // LANES
    full = u_range // LANES
    row_lane, row_sub = tile_rows.reshape(1, slots), tile_rows.reshape(slots, 1)
    col_lane, col_sub = tile_cols.reshape(1, slots), tile_cols.reshape(slots, 1)
    own = lax.axis_index(COL).reshape(1)
    products = [pltpu.VMEM((slots, size), F32), pltpu.VMEM((slots, size), F32)]

    u_blocks = pl.pallas_call(
        regroup_kernel,
        name="regroup",
        grid=(cols_n,),
        in_specs=[pl.BlockSpec((u_here, u_own), lambda k: (0, k))],
        out_specs=pl.BlockSpec((1, u_here, u_own), lambda k: (k, 0, 0)),
        out_shape=jax.ShapeDtypeStruct((cols_n, u_here, u_own), F32),
    )(u_start)
    u_got = swapped(u_blocks, COL).reshape(-1, u_own)
    u_kept, u_gram = call(kept_kernel, "left_kept", [(keep, u_own), (8, LANES)], [u_got, keep_u])
    u_wide = lax.all_gather(u_kept, COL, axis=0)

    v_blocks = jnp.moveaxis(v_start.reshape(v_here, rows_n, v_own), 1, 0)
    v_got = swapped(v_blocks, ROW).reshape(-1, v_own)
    next_rows = v_next.reshape(v_rows, LANES)
    v_kept, message = call(
        kept_with_kernel,
        "right_kept",
        [(keep, v_own), (devices, 8, LANES)],
        [v_got, keep_v, next_rows],
        scratch=[pltpu.VMEM((LANES, v_own), F32)],
    )
    got = swapped(message, ROW_COL)
    v_0, gram_v, message = call(
        functools.partial(first_kernel, v_length),
        "first_right",
        [(v_rows, LANES), (PAD, LANES), (rows_n, v_rows, LANES)],
        [got, v_kept, next_rows],
    )

    def forward(message, extra):
        got = swapped(message, ROW)
        (message,) = call(
            functools.partial(forward_kernel, bool(extra)),
            "forward",
            [(cols_n, full + 8 * len(extra), LANES)],
            [got, tile_blocks, col_sub, row_lane, tile_count, *extra],
            scalars=(4,),
            scratch=products,
        )
        return swapped(message, COL)

    def left(got, m, gram, others):
        first = gram is None
        image, message = call(
            functools.partial(left_dots_kernel, u_length),
            "left_dots",
            [(full, LANES), (rows_n, 16, LANES) if first else (rows_n, LANES)],
            [got, u_wide, *others],
        )
        got = swapped(message, ROW)
        known = [] if first else [gram]
        new, own_new, gram, scale, message = call(
            functools.partial(left_kernel, m),
            "left",
            [(full, LANES), (u_rows, LANES), (PAD, LANES), (1, LANES), (rows_n, v_rows, LANES)],
            [got, image, u_wide, tile_blocks, row_sub, col_lane, tile_count, own, *known, *others],
            scalars=(6, 7),
            scratch=products,
        )
        return new, own_new, gram, scale, swapped(message, ROW)

    def right_dots(got, others):
        image, message = call(
            functools.partial(right_dots_kernel, v_length),
            "right_dots",
            [(v_rows, LANES), (devices, LANES)],
            [got, v_kept, *others],
        )
        return image, swapped(message, ROW_COL)

    got = forward(message, [u_gram])
    u_0_wide, u_0, gram_u, alpha_0, got = left(got, keep, None, [])
    image, got = right_dots(got, [v_0])
    v_1, gram_v, beta_0, message = call(
        functools.partial(right_kernel, keep + 1),
        "right",
        [(v_rows, LANES), (PAD, LANES), (1, LANES), (rows_n, v_rows, LANES)],
        [got, image, v_kept, gram_v, v_0],
    )
    got = forward(message, [])
    _, u_1, gram_u, alpha_1, got = left(got, keep + 1, gram_u, [u_0_wide])
    (u_basis,) = call(left_out_kernel, "left_out", [(keep + 2, u_own)], [u_kept, u_0, u_1])
    image, got = right_dots(got, [v_0, v_1])
    v_basis, scales = call(
        functools.partial(last_kernel, keep + 2),
        "last_right",
        [(keep + 3, v_own), (2, 2)],
        [got, image, v_kept, gram_v, v_0, v_1, alpha_0, alpha_1, beta_0],
    )
    return u_basis, v_basis, scales


def solution(mesh):
    finer = Mesh(mesh.devices.reshape(2, 4, 2, 2, 4), ROW_COL)
    return jax.shard_map(
        per_device,
        mesh=finer,
        in_specs=(
            P(COL, ROW),
            P(ROW, COL),
            P(),
            P(),
            P(COL_ROW),
            P(ROW_COL, None, None),
            P(ROW_COL),
            P(ROW_COL),
            P(ROW_COL),
        ),
        out_specs=(P(None, ROW_COL), P(None, COL_ROW), P()),
        check_vma=False,
    )
```

```python
import functools

import jax
import jax.numpy as jnp
from jax import lax
from jax.experimental import pallas as pl
from jax.experimental.pallas import tpu as pltpu
from jax.sharding import Mesh
from jax.sharding import PartitionSpec as P

ROW = ("row_0", "row_1", "row_2")
COL = ("col_0", "col_1")
ROW_COL = ROW + COL
COL_ROW = COL + ROW

HIGH = lax.Precision.HIGHEST
F32 = jnp.float32
BF16 = jnp.bfloat16
LANES = 128
PAD = 48
EPS = 1e-06
VMEM_LIMIT = 24 << 20
CHUNKS = 8


def swapped(blocks, axis):
    return lax.all_to_all(blocks, axis, 0, 0, tiled=True)


def iota(shape, dim):
    return lax.broadcasted_iota(jnp.int32, shape, dim)


def as_row(col):
    spot = iota((PAD, LANES), 0) == iota((PAD, LANES), 1)
    return jnp.sum(jnp.where(spot, col, 0.0), axis=0, keepdims=True)


def as_col(row):
    spot = iota((PAD, LANES), 0) == iota((PAD, LANES), 1)
    return jnp.sum(jnp.where(spot, row, 0.0), axis=1, keepdims=True)


def total(x):
    return jnp.sum(jnp.sum(x, axis=1, keepdims=True), axis=0, keepdims=True)


def packed(gram, n):
    width = n // 2 + 1
    twice = gram + pltpu.roll(gram, n, 1)
    turned, sub = twice, iota((PAD, LANES), 0)
    for bit in (1, 2, 4, 8, 16, 32):
        turned = jnp.where(sub & bit != 0, pltpu.roll(turned, LANES - bit, 1), turned)
    turned = jnp.where(iota((PAD, LANES), 1) < width, turned, 0.0)
    out = turned[0:8]
    for g in range(1, PAD // 8):
        out = out + pltpu.roll(turned[8 * g : 8 * g + 8], width * g, 1)
    return out


def unpacked(pack, n):
    width = n // 2 + 1
    groups = [pack] + [
        pltpu.roll(pack, LANES - width * g, 1) for g in range(1, PAD // 8)
    ]
    turned = jnp.concatenate(groups, axis=0)
    turned = jnp.where(iota((PAD, LANES), 1) < width, turned, 0.0)
    wide = pltpu.roll(turned, 0, 1, stride=1, stride_axis=0)
    half = wide + pltpu.roll(wide, LANES - n, 1)
    lane, sub = iota((PAD, LANES), 1), iota((PAD, LANES), 0)
    half = jnp.where((lane < n) & (sub < n), half, 0.0)
    square = jnp.concatenate([half, jnp.zeros((LANES - PAD, LANES), F32)], axis=0)
    return half + jnp.where(lane == sub, 0.0, square.T[:PAD])


def solve(gram, dots_col, square, m):
    coef_col = 2.0 * dots_col - jnp.sum(gram * as_row(dots_col), axis=1, keepdims=True)
    across = dots_col - jnp.sum(gram * as_row(coef_col), axis=1, keepdims=True)
    mean_square = square - total(coef_col * (dots_col + across))
    mean_square = jnp.maximum(mean_square, 0.0)
    scale = jnp.sqrt(mean_square + EPS)
    inverse = 1.0 / scale
    across = across * inverse
    lane, sub = iota((PAD, LANES), 1), iota((PAD, LANES), 0)
    grown = jnp.where(sub == m, as_row(across), gram)
    grown = jnp.where(lane == m, across, grown)
    grown = jnp.where((lane == m) & (sub == m), mean_square * inverse * inverse, grown)
    return coef_col, scale, inverse, grown


def at(value, index):
    return jnp.where(iota((PAD, 1), 0) == index, value, 0.0)


def padded(col):
    return jnp.concatenate([col, jnp.zeros((PAD - col.shape[0], 1), F32)], axis=0)


def prepare_kernel(
    count_ref, own_u_ref, own_v_ref, start_ref, rows_ref, cols_ref, keep_u_ref, keep_v_ref, next_ref,
    out_ref, keep_u_out, keep_v_out, next_out, row_lane_ref, col_lane_ref, row_sub_ref, col_sub_ref,
    index_ref, sems,
):
    blocks, _, width = out_ref.shape
    pairs = [(start_ref.at[:, k * width : (k + 1) * width], out_ref.at[k]) for k in range(blocks)]
    pairs += [(keep_u_ref, keep_u_out), (keep_v_ref, keep_v_out), (next_ref, next_out)]
    pairs += [(rows_ref, index_ref.at[0]), (cols_ref, index_ref.at[1])]
    copies = [pltpu.make_async_copy(a, b, sems.at[n]) for n, (a, b) in enumerate(pairs)]
    for copy in copies:
        copy.start()
    for copy in copies[::-1]:
        copy.wait()
    slots = rows_ref.shape[1]
    double = 2 * slots
    pair = iota((double, slots), 0) // 2 == iota((double, slots), 1)
    spot = iota((double, double), 0) == iota((double, double), 1)
    used = iota((1, double), 1) // 2 < count_ref[0]
    for n, (lane_ref, sub_ref) in enumerate(((row_lane_ref, row_sub_ref), (col_lane_ref, col_sub_ref))):
        sub = jnp.sum(jnp.where(pair, index_ref[n].astype(F32), 0.0), axis=1, keepdims=True)
        sub_ref[...] = sub
        lane = jnp.sum(jnp.where(spot, sub, 0.0), axis=0, keepdims=True)
        lane_ref[...] = jnp.where(used, lane, -1.0)


def kept_kernel(start_ref, keep_ref, out_ref, gram_ref):
    basis = jnp.dot(keep_ref[...], start_ref[...], precision=HIGH, preferred_element_type=F32)
    out_ref[...] = basis
    rows = basis.shape[0]
    wide = jnp.concatenate([basis, jnp.zeros((PAD - rows, basis.shape[1]), F32)], axis=0)
    full = jnp.concatenate([wide, jnp.zeros((LANES - PAD, basis.shape[1]), F32)], axis=0)
    gram = lax.dot_general(
        wide, full, (((1,), (1,)), ((), ())), precision=HIGH, preferred_element_type=F32
    )
    gram_ref[...] = packed(gram, rows + 1)


def kept_with_kernel(start_ref, keep_ref, next_ref, out_ref, message_ref, wide_ref):
    basis = jnp.dot(keep_ref[...], start_ref[...], precision=HIGH, preferred_element_type=F32)
    out_ref[...] = basis
    rows = basis.shape[0]
    wide_ref[...] = jnp.zeros_like(wide_ref)
    wide_ref[:rows] = basis
    for j in range(next_ref.shape[0]):
        wide_ref[rows : rows + 1, j * LANES : (j + 1) * LANES] = next_ref[j : j + 1]
    full = wide_ref[...]
    gram = lax.dot_general(
        full[:PAD], full, (((1,), (1,)), ((), ())), precision=HIGH, preferred_element_type=F32
    )
    message_ref[...] = jnp.broadcast_to(packed(gram, rows + 1)[None], message_ref.shape)


def projected_slice(vector_ref, basis_ref, coef_col):
    count = basis_ref.shape[0]
    rows = []
    for j in range(vector_ref.shape[0]):
        part = basis_ref[:, j * LANES : (j + 1) * LANES] * coef_col[:count]
        rows.append(jnp.sum(part, axis=0, keepdims=True))
    return vector_ref[...] - jnp.concatenate(rows, axis=0)


def first_kernel(length, got_ref, basis_ref, next_ref, vector_ref, gram_ref, message_ref):
    count = basis_ref.shape[0]
    gram = unpacked(jnp.sum(got_ref[...], axis=0), count + 1) * (1.0 / length)
    lane, sub = iota((PAD, LANES), 1), iota((PAD, LANES), 0)
    dots = jnp.sum(jnp.where((lane == count) & (sub < count), gram, 0.0), axis=1, keepdims=True)
    square = total(jnp.where((lane == count) & (sub == count), gram, 0.0))
    gram = jnp.where((lane < count) & (sub < count), gram, 0.0)
    coef, scale, inverse, grown = solve(gram, dots, square, count)
    new = projected_slice(next_ref, basis_ref, coef) * inverse
    vector_ref[...] = new
    gram_ref[...] = grown
    message_ref[...] = jnp.broadcast_to(new[None], message_ref.shape)


def started(source, target, sems):
    parts = sems.shape[0]
    step = source.shape[0] // parts
    copies = [
        pltpu.make_async_copy(
            source.at[n * step : (n + 1) * step], target.at[n * step : (n + 1) * step], sems.at[n]
        )
        for n in range(parts)
    ]
    for copy in copies:
        copy.start()
    return copies


def multiplied(forward, both, entries, tiles_ref, tile_copies, pick_ref, put_ref, picked_ref, product_ref):
    slots, size = tiles_ref.shape[:2]
    blocks = size // LANES
    rows = entries.shape[0]
    high = entries.astype(BF16)
    low = (entries - high.astype(F32)).astype(BF16)
    lane, part = iota((2 * slots, rows), 1).astype(F32), iota((2 * slots, rows), 0) % 2
    for b in range(blocks):
        spot = lane == blocks * pick_ref[...] + b
        picked = jnp.dot((spot & (part == 0)).astype(BF16), high, preferred_element_type=F32)
        if both:
            picked = picked + jnp.dot((spot & (part == 1)).astype(BF16), low, preferred_element_type=F32)
        picked_ref[:, b * LANES : (b + 1) * LANES] = picked
    for t in range(slots):
        if tile_copies and t % (slots // CHUNKS) == 0:
            tile_copies[t // (slots // CHUNKS)].wait()
        product_ref[2 * t : 2 * t + 2] = lax.dot_general(
            picked_ref[2 * t : 2 * t + 2].astype(BF16),
            tiles_ref[t],
            (((1,), (1 if forward else 0,)), ((), ())),
            preferred_element_type=F32,
        )
    sub = iota((rows, 2 * slots), 0).astype(F32)
    out = None
    for b in range(blocks):
        hot = (sub == blocks * put_ref[...] + b).astype(F32)
        part = jnp.dot(
            hot, product_ref[:, b * LANES : (b + 1) * LANES], precision=HIGH, preferred_element_type=F32
        )
        out = part if out is None else out + part
    return out


def first_forward_kernel(
    got_ref, tiles_hbm, pick_ref, put_ref, gram_ref, message_ref, picked_ref, product_ref, tile_sems, tiles_ref
):
    copies = started(tiles_hbm, tiles_ref, tile_sems)
    entries = got_ref[...].reshape(-1, LANES)
    sums = multiplied(True, False, entries, tiles_ref, copies, pick_ref, put_ref, picked_ref, product_ref).astype(BF16)
    rows = sums.shape[0]
    gram = gram_ref[...]
    high = gram.astype(BF16).astype(F32)
    middle = (gram - high).astype(BF16).astype(F32)
    low = gram - high - middle
    first = jnp.concatenate([high, middle], axis=0).astype(BF16)
    second = jnp.concatenate([low, jnp.zeros_like(low)], axis=0).astype(BF16)
    for k in range(message_ref.shape[0]):
        message_ref[k, :rows] = sums
        message_ref[k, rows : rows + 16] = first
        message_ref[k, rows + 16 : rows + 32] = second


def dots_kernel(length, fetch, got_ref, wide_ref, *refs):
    copies = []
    if fetch:
        *others, image_ref, message_ref, near_ref, wide_sems = refs
        copies = started(wide_ref, near_ref, wide_sems)
        wide_ref = near_ref
    else:
        *others, image_ref, message_ref = refs
    first = got_ref.shape[1] > LANES
    image = jnp.sum(got_ref[:, :LANES].astype(F32), axis=0)
    image_ref[...] = image
    parts, count, width = wide_ref.shape
    across = width // LANES
    acc = jnp.zeros((count, LANES), F32)
    for k in range(parts):
        if copies and k % (parts // CHUNKS) == 0:
            copies[k // (parts // CHUNKS)].wait()
        for j in range(across):
            r = k * across + j
            acc = acc + wide_ref[k, :, j * LANES : (j + 1) * LANES] * image_ref[r : r + 1]
    dots = padded(jnp.sum(acc, axis=1, keepdims=True))
    for n, other in enumerate(others):
        dots = dots + at(total(other[...].reshape(image.shape) * image), count + n)
    dots = dots + at(total(image * image), PAD - 1)
    row = as_row(dots) * (1.0 / length)
    if first:
        grams = jnp.sum(got_ref[:, LANES:].astype(F32), axis=0)
        gram = (grams[:8] + grams[8:16] + grams[16:24]) * (1.0 / length)
        message_ref[:, :8] = jnp.broadcast_to(gram[None], (message_ref.shape[0], 8, LANES))
        message_ref[:, 8:] = jnp.broadcast_to(row[None], (message_ref.shape[0], 8, LANES))
    else:
        message_ref[...] = jnp.broadcast_to(row, message_ref.shape)


def split_dots(row):
    col = as_col(row)
    last = iota((PAD, 1), 0) == PAD - 1
    return jnp.where(last, 0.0, col), total(jnp.where(last, col, 0.0))


def vector_kernel(
    m, forward, known, fetch, own_ref, got_ref, image_ref, wide_ref, tiles_ref, pick_ref, put_ref, *refs
):
    copies = []
    if fetch:
        *refs, near_ref, picked_ref, product_ref, tile_sems = refs if fetch == "keep" else refs[:-4] + refs[-1:] + refs[-4:-1]
        copies = started(tiles_ref, near_ref, tile_sems)
        tiles_ref = near_ref
    else:
        *refs, picked_ref, product_ref = refs
    *inputs, new_ref, own_out_ref, gram_ref, scale_ref, message_ref = refs
    parts, count, width = wide_ref.shape
    if known:
        gram = inputs[0][...]
        row = jnp.sum(got_ref[...], axis=0, keepdims=True)
        others = inputs[1:]
    else:
        got = jnp.sum(got_ref[...], axis=0)
        gram = unpacked(got[:8], count + 1)
        row = got[8:9]
        others = inputs
    dots, square = split_dots(row)
    coef, scale, inverse, grown = solve(gram, dots, square, m)
    gram_ref[...] = grown
    scale_ref[...] = jnp.broadcast_to(scale, scale_ref.shape)
    across = width // LANES
    by_lane = jnp.broadcast_to(coef[:count], (count, LANES))
    for k in range(parts):
        sums = [
            jnp.sum(wide_ref[k, :, j * LANES : (j + 1) * LANES] * by_lane, axis=0, keepdims=True)
            for j in range(across)
        ]
        span = slice(k * across, (k + 1) * across)
        new_ref[span] = image_ref[span] - jnp.concatenate(sums, axis=0)
    new = new_ref[...]
    for n, other in enumerate(others):
        new = new - coef[count + n : count + n + 1] * other[...].reshape(new.shape)
    new = new * inverse
    new_ref[...] = new
    own_out_ref[...] = new_ref[pl.ds(pl.multiple_of(own_ref[0] * across, across), across)]
    sums = multiplied(forward, True, new, tiles_ref, copies, pick_ref, put_ref, picked_ref, product_ref)
    if message_ref.shape[1] == sums.shape[0]:
        message_ref[...] = jnp.broadcast_to(sums.astype(message_ref.dtype)[None], message_ref.shape)
    else:
        message_ref[...] = sums.reshape(message_ref.shape)


def right_dots_kernel(length, got_ref, basis_ref, *refs):
    refs = list(refs)
    image_ref, message_ref = refs[-2:]
    others = refs[:-2]
    image = jnp.sum(got_ref[...], axis=0)
    image_ref[...] = image
    count = basis_ref.shape[0]
    acc = jnp.zeros((count, LANES), F32)
    for j in range(image.shape[0]):
        acc = acc + basis_ref[:, j * LANES : (j + 1) * LANES] * image_ref[j : j + 1]
    dots = padded(jnp.sum(acc, axis=1, keepdims=True))
    for n, other in enumerate(others):
        dots = dots + at(total(other[...] * image), count + n)
    dots = dots + at(total(image * image), PAD - 1)
    message_ref[...] = jnp.broadcast_to(as_row(dots) * (1.0 / length), message_ref.shape)


def new_right(m, got_ref, image_ref, basis_ref, gram_ref, others):
    count = basis_ref.shape[0]
    dots, square = split_dots(jnp.sum(got_ref[...], axis=0, keepdims=True))
    coef, scale, inverse, grown = solve(gram_ref[...], dots, square, m)
    new = projected_slice(image_ref, basis_ref, coef)
    for n, other in enumerate(others):
        new = new - coef[count + n : count + n + 1] * other[...]
    return new * inverse, scale, grown


def put_rows(out_ref, row, vector):
    for j in range(vector.shape[0]):
        out_ref[row : row + 1, j * LANES : (j + 1) * LANES] = vector[j : j + 1]


def last_kernel(
    m, got_ref, image_ref, basis_ref, gram_ref, old_0_ref, old_1_ref,
    alpha_0_ref, alpha_1_ref, beta_0_ref, out_ref, scales_ref,
):
    new, scale, _ = new_right(m, got_ref, image_ref, basis_ref, gram_ref, [old_0_ref, old_1_ref])
    count = basis_ref.shape[0]
    out_ref[:count] = basis_ref[...]
    put_rows(out_ref, count, old_0_ref[...])
    put_rows(out_ref, count + 1, old_1_ref[...])
    put_rows(out_ref, count + 2, new)
    lane = iota((1, LANES), 1)
    alphas = jnp.where(lane == 0, alpha_0_ref[...], alpha_1_ref[...])
    betas = jnp.where(lane == 0, beta_0_ref[...], jnp.broadcast_to(scale, (1, LANES)))
    scales_ref[...] = jnp.concatenate([alphas, betas], axis=0)[:, :2]


def left_out_kernel(basis_ref, new_0_ref, new_1_ref, out_ref):
    count = basis_ref.shape[0]
    out_ref[:count] = basis_ref[...]
    put_rows(out_ref, count, new_0_ref[...])
    put_rows(out_ref, count + 1, new_1_ref[...])


WHOLE = pl.BlockSpec(memory_space=pltpu.VMEM)
SCALAR = pl.BlockSpec(memory_space=pltpu.SMEM)
FAR = pl.BlockSpec(memory_space=pltpu.HBM)


def in_hbm(x):
    return pltpu.with_memory_space_constraint(x, pltpu.HBM)


def in_vmem(x):
    return pltpu.with_memory_space_constraint(x, pltpu.VMEM)


def call(kernel, name, outs, args, scalars=(), scratch=(), far=(), near=()):
    shapes = tuple(jax.ShapeDtypeStruct(s, F32) if isinstance(s, tuple) else s for s in outs)
    specs = [SCALAR if i in scalars else FAR if i in far else WHOLE for i in range(len(args))]
    return pl.pallas_call(
        kernel,
        name=name,
        out_shape=shapes,
        in_specs=specs,
        out_specs=tuple(WHOLE for _ in shapes),
        scratch_shapes=list(scratch),
        compiler_params=pltpu.CompilerParams(vmem_limit_bytes=VMEM_LIMIT),
    )(*(in_hbm(x) if i in far else in_vmem(x) if i in near else x for i, x in enumerate(args)))


def after(x, *earlier):
    return lax.optimization_barrier((x, *earlier))[0]


def per_device(
    u_start, v_start, keep_u, keep_v, v_next, tile_blocks, tile_rows, tile_cols, tile_count
):
    rows_n, cols_n = lax.axis_size(ROW), lax.axis_size(COL)
    devices = rows_n * cols_n
    keep = keep_u.shape[1]
    slots, size = tile_blocks.shape[:2]
    u_here, u_range = u_start.shape
    v_here, v_range = v_start.shape
    u_own, v_own = u_range // cols_n, v_range // rows_n
    u_length, v_length = u_range * rows_n, v_range * cols_n
    u_rows, v_rows = u_own // LANES, v_own // LANES
    u_full, v_full = u_range // LANES, v_range // LANES
    products = [pltpu.VMEM((2 * slots, size), F32), pltpu.VMEM((2 * slots, size), F32)]
    sems = [pltpu.SemaphoreType.DMA((CHUNKS,))]
    narrow = functools.partial(jax.ShapeDtypeStruct, dtype=BF16)

    own_u, own_v = lax.axis_index(COL).reshape(1), lax.axis_index(ROW).reshape(1)
    u_blocks, keep_u, keep_v, next_rows, row_lane, col_lane, row_sub, col_sub = call(
        prepare_kernel,
        "prepare",
        [
            (cols_n, u_here, u_own),
            keep_u.T.shape,
            keep_v.T.shape,
            (v_rows, LANES),
            (1, 2 * slots),
            (1, 2 * slots),
            (2 * slots, 1),
            (2 * slots, 1),
        ],
        [
            tile_count,
            own_u,
            own_v,
            u_start,
            tile_rows.reshape(1, slots),
            tile_cols.reshape(1, slots),
            keep_u.T,
            keep_v.T,
            v_next.reshape(v_rows, LANES),
        ],
        scalars=(0, 1, 2),
        scratch=[pltpu.VMEM((2, 1, slots), jnp.int32), pltpu.SemaphoreType.DMA((cols_n + 5,))],
        far=range(3, 9),
    )
    u_got = swapped(u_blocks, COL).reshape(-1, u_own)
    u_kept, u_gram = call(kept_kernel, "left_kept", [(keep, u_own), (8, LANES)], [u_got, keep_u])
    u_wide = lax.all_gather(u_kept, COL, axis=0)

    v_blocks = after(jnp.moveaxis(v_start.reshape(v_here, rows_n, v_own), 1, 0), u_kept)
    v_got = swapped(v_blocks, ROW).reshape(-1, v_own)
    v_kept, message = call(
        kept_with_kernel,
        "right_kept",
        [(keep, v_own), (devices, 8, LANES)],
        [v_got, keep_v, next_rows],
        scratch=[pltpu.VMEM((LANES, v_own), F32)],
    )
    v_wide = lax.all_gather(v_kept, ROW, axis=0)
    got = swapped(message, ROW_COL)
    v_0, gram_v, message = call(
        functools.partial(first_kernel, v_length),
        "first_right",
        [(v_rows, LANES), (PAD, LANES), (rows_n, v_rows, LANES)],
        [got, v_kept, next_rows],
    )
    v_0_wide = swapped(message, ROW)
    tile_room = [pltpu.VMEM(tile_blocks.shape, BF16)]
    (message,) = call(
        first_forward_kernel,
        "forward",
        [narrow((cols_n, u_full + 32, LANES))],
        [v_0_wide, tile_blocks, col_sub, row_lane, u_gram],
        scratch=products + sems + tile_room,
        far=(1,),
    )
    got = swapped(message, COL)

    def wide_dots(got, wide, others, length, name, image, dots):
        return call(
            functools.partial(dots_kernel, length, True),
            name,
            [image, dots, pltpu.VMEM(wide.shape, F32)],
            [got, wide, *others],
            scratch=sems,
            far=(1,),
        )

    def left(dots, image, wide, tiles, m, gram, others, message):
        known = [] if gram is None else [gram]
        return call(
            functools.partial(vector_kernel, m, False, bool(known), None if known else "once"),
            "left",
            [(u_full, LANES), (u_rows, LANES), (PAD, LANES), (1, LANES), message],
            [own_u, swapped(dots, ROW), image, wide, tiles, row_sub, col_lane, *known, *others],
            scalars=(0,),
            scratch=products if known else products + sems + tile_room,
            near=(3, 4) if known else (3,),
            far=() if known else (4,),
        )

    image, dots, u_near = wide_dots(got, u_wide, [], u_length, "left_dots", (u_full, LANES), (rows_n, 16, LANES))
    u_0_wide, u_0, gram_u, alpha_0, message = left(
        dots, image, u_near, tile_blocks, keep, None, [], narrow((rows_n, v_full, LANES))
    )
    image, dots, v_near = wide_dots(
        swapped(message, ROW), v_wide, [v_0_wide], v_length, "right_dots", (v_full, LANES), (cols_n, LANES)
    )
    _, v_1, gram_v, beta_0, message, tiles = call(
        functools.partial(vector_kernel, keep + 1, True, True, "keep"),
        "right",
        [(v_full, LANES), (v_rows, LANES), (PAD, LANES), (1, LANES), narrow((cols_n, u_full, LANES)), *tile_room],
        [own_v, swapped(dots, COL), image, v_near, tile_blocks, col_sub, row_lane, gram_v, v_0_wide],
        scalars=(0,),
        scratch=products + sems,
        near=(3,),
        far=(4,),
    )
    got = swapped(message, COL)
    image, dots = call(
        functools.partial(dots_kernel, u_length, False),
        "left_dots",
        [(u_full, LANES), (rows_n, LANES)],
        [got, u_near, u_0_wide],
        near=(1,),
    )
    _, u_1, _, alpha_1, message = left(
        dots, image, u_near, tiles, keep + 1, gram_u, [u_0_wide], (rows_n, v_rows, LANES)
    )
    got = swapped(message, ROW)
    (u_basis,) = call(left_out_kernel, "left_out", [(keep + 2, u_own)], [u_kept, u_0, u_1])
    image, dots = call(
        functools.partial(right_dots_kernel, v_length),
        "last_dots",
        [(v_rows, LANES), (devices, LANES)],
        [got, v_kept, v_0, v_1],
    )
    v_basis, scales = call(
        functools.partial(last_kernel, keep + 2),
        "last_right",
        [(keep + 3, v_own), (2, 2)],
        [swapped(dots, ROW_COL), image, v_kept, gram_v, v_0, v_1, alpha_0, alpha_1, beta_0],
    )
    return u_basis, v_basis, scales


def solution(mesh):
    finer = Mesh(mesh.devices.reshape(2, 4, 2, 2, 4), ROW_COL)
    return jax.shard_map(
        per_device,
        mesh=finer,
        in_specs=(
            P(COL, ROW),
            P(ROW, COL),
            P(),
            P(),
            P(COL_ROW),
            P(ROW_COL, None, None),
            P(ROW_COL),
            P(ROW_COL),
            P(ROW_COL),
        ),
        out_specs=(P(None, ROW_COL), P(None, COL_ROW), P()),
        check_vma=False,
    )
```

```python
import functools

import jax
import jax.numpy as jnp
from jax import lax
from jax.experimental import pallas as pl
from jax.experimental.pallas import tpu as pltpu
from jax.sharding import Mesh
from jax.sharding import PartitionSpec as P

ROW = ("row_0", "row_1", "row_2")
COL = ("col_0", "col_1")
ROW_COL = ROW + COL
COL_ROW = COL + ROW

HIGH = lax.Precision.HIGHEST
F32 = jnp.float32
BF16 = jnp.bfloat16
LANES = 128
PAD = 48
PLACES = 4
EPS = 1e-06
VMEM_LIMIT = 24 << 20
CHUNKS = 8


def swapped(blocks, axis):
    return lax.all_to_all(blocks, axis, 0, 0, tiled=True)


def iota(shape, dim):
    return lax.broadcasted_iota(jnp.int32, shape, dim)


def as_row(col):
    spot = iota((PAD, LANES), 0) == iota((PAD, LANES), 1)
    return jnp.sum(jnp.where(spot, col, 0.0), axis=0, keepdims=True)


def as_col(row):
    spot = iota((PAD, LANES), 0) == iota((PAD, LANES), 1)
    return jnp.sum(jnp.where(spot, row, 0.0), axis=1, keepdims=True)


def total(x):
    return jnp.sum(jnp.sum(x, axis=1, keepdims=True), axis=0, keepdims=True)


def packed(gram, n):
    width = n // 2 + 1
    twice = gram + pltpu.roll(gram, n, 1)
    turned, sub = twice, iota((PAD, LANES), 0)
    for bit in (1, 2, 4, 8, 16, 32):
        turned = jnp.where(sub & bit != 0, pltpu.roll(turned, LANES - bit, 1), turned)
    turned = jnp.where(iota((PAD, LANES), 1) < width, turned, 0.0)
    out = turned[0:8]
    for g in range(1, PAD // 8):
        out = out + pltpu.roll(turned[8 * g : 8 * g + 8], width * g, 1)
    return out


def unpacked(pack, n):
    width = n // 2 + 1
    groups = [pack] + [
        pltpu.roll(pack, LANES - width * g, 1) for g in range(1, PAD // 8)
    ]
    turned = jnp.concatenate(groups, axis=0)
    turned = jnp.where(iota((PAD, LANES), 1) < width, turned, 0.0)
    wide = pltpu.roll(turned, 0, 1, stride=1, stride_axis=0)
    half = wide + pltpu.roll(wide, LANES - n, 1)
    lane, sub = iota((PAD, LANES), 1), iota((PAD, LANES), 0)
    half = jnp.where((lane < n) & (sub < n), half, 0.0)
    square = jnp.concatenate([half, jnp.zeros((LANES - PAD, LANES), F32)], axis=0)
    return half + jnp.where(lane == sub, 0.0, square.T[:PAD])


def solve(gram, dots_col, square, m):
    coef_col = 2.0 * dots_col - jnp.sum(gram * as_row(dots_col), axis=1, keepdims=True)
    across = dots_col - jnp.sum(gram * as_row(coef_col), axis=1, keepdims=True)
    mean_square = square - total(coef_col * (dots_col + across))
    mean_square = jnp.maximum(mean_square, 0.0)
    scale = jnp.sqrt(mean_square + EPS)
    inverse = 1.0 / scale
    across = across * inverse
    lane, sub = iota((PAD, LANES), 1), iota((PAD, LANES), 0)
    grown = jnp.where(sub == m, as_row(across), gram)
    grown = jnp.where(lane == m, across, grown)
    grown = jnp.where((lane == m) & (sub == m), mean_square * inverse * inverse, grown)
    return coef_col, scale, inverse, grown


def at(value, index):
    return jnp.where(iota((PAD, 1), 0) == index, value, 0.0)


def padded(col):
    return jnp.concatenate([col, jnp.zeros((PAD - col.shape[0], 1), F32)], axis=0)


def prepare_kernel(
    count_ref, own_ref, start_ref, rows_ref, cols_ref, keep_u_ref, keep_v_ref, next_ref,
    out_ref, keep_u_out, keep_v_out, next_out, row_lane_ref, col_lane_ref, row_sub_ref, col_sub_ref,
    index_ref, sems,
):
    blocks, _, width = out_ref.shape
    pairs = [(start_ref.at[:, k * width : (k + 1) * width], out_ref.at[k]) for k in range(blocks)]
    pairs += [(keep_u_ref, keep_u_out), (keep_v_ref, keep_v_out), (next_ref, next_out)]
    pairs += [(rows_ref, index_ref.at[0]), (cols_ref, index_ref.at[1])]
    copies = [pltpu.make_async_copy(a, b, sems.at[n]) for n, (a, b) in enumerate(pairs)]
    for copy in copies:
        copy.start()
    for copy in copies[::-1]:
        copy.wait()
    slots = rows_ref.shape[1]
    double = 2 * slots
    pair = iota((double, slots), 0) // 2 == iota((double, slots), 1)
    spot = iota((double, double), 0) == iota((double, double), 1)
    used = iota((1, double), 1) // 2 < count_ref[0]
    for n, (lane_ref, sub_ref) in enumerate(((row_lane_ref, row_sub_ref), (col_lane_ref, col_sub_ref))):
        sub = jnp.sum(jnp.where(pair, index_ref[n].astype(F32), 0.0), axis=1, keepdims=True)
        sub_ref[...] = sub
        lane = jnp.sum(jnp.where(spot, sub, 0.0), axis=0, keepdims=True)
        lane_ref[...] = jnp.where(used, lane, -1.0)


def kept_kernel(start_ref, keep_ref, out_ref, gram_ref):
    basis = jnp.dot(keep_ref[...], start_ref[...], precision=HIGH, preferred_element_type=F32)
    out_ref[...] = basis
    rows = basis.shape[0]
    wide = jnp.concatenate([basis, jnp.zeros((PAD - rows, basis.shape[1]), F32)], axis=0)
    full = jnp.concatenate([wide, jnp.zeros((LANES - PAD, basis.shape[1]), F32)], axis=0)
    gram = lax.dot_general(
        wide, full, (((1,), (1,)), ((), ())), precision=HIGH, preferred_element_type=F32
    )
    gram_ref[...] = packed(gram, rows + 1)


def kept_with_kernel(start_ref, keep_ref, next_ref, out_ref, message_ref, wide_ref):
    basis = jnp.dot(keep_ref[...], start_ref[...], precision=HIGH, preferred_element_type=F32)
    out_ref[...] = basis
    rows = basis.shape[0]
    wide_ref[...] = jnp.zeros_like(wide_ref)
    wide_ref[:rows] = basis
    for j in range(next_ref.shape[0]):
        wide_ref[rows : rows + 1, j * LANES : (j + 1) * LANES] = next_ref[j : j + 1]
    full = wide_ref[...]
    gram = lax.dot_general(
        full[:PAD], full, (((1,), (1,)), ((), ())), precision=HIGH, preferred_element_type=F32
    )
    message_ref[...] = jnp.broadcast_to(packed(gram, rows + 1)[None], message_ref.shape)


def projected_slice(vector_ref, basis_ref, coef_col):
    count = basis_ref.shape[0]
    rows = []
    for j in range(vector_ref.shape[0]):
        part = basis_ref[:, j * LANES : (j + 1) * LANES] * coef_col[:count]
        rows.append(jnp.sum(part, axis=0, keepdims=True))
    return vector_ref[...] - jnp.concatenate(rows, axis=0)


def first_kernel(length, got_ref, basis_ref, next_ref, vector_ref, gram_ref, message_ref):
    count = basis_ref.shape[0]
    gram = unpacked(jnp.sum(got_ref[...], axis=0), count + 1) * (1.0 / length)
    lane, sub = iota((PAD, LANES), 1), iota((PAD, LANES), 0)
    dots = jnp.sum(jnp.where((lane == count) & (sub < count), gram, 0.0), axis=1, keepdims=True)
    square = total(jnp.where((lane == count) & (sub == count), gram, 0.0))
    gram = jnp.where((lane < count) & (sub < count), gram, 0.0)
    coef, scale, inverse, grown = solve(gram, dots, square, count)
    new = projected_slice(next_ref, basis_ref, coef) * inverse
    vector_ref[...] = new
    gram_ref[...] = grown
    message_ref[...] = jnp.broadcast_to(new[None], message_ref.shape)


def started(source, target, sems):
    parts = sems.shape[0]
    step = source.shape[0] // parts
    copies = [
        pltpu.make_async_copy(
            source.at[n * step : (n + 1) * step], target.at[n * step : (n + 1) * step], sems.at[n]
        )
        for n in range(parts)
    ]
    for copy in copies:
        copy.start()
    return copies


def multiplied(forward, both, entries, tiles_ref, tile_copies, pick_ref, put_ref, picked_ref, product_ref):
    slots, size = tiles_ref.shape[:2]
    blocks = size // LANES
    rows = entries.shape[0]
    high = entries.astype(BF16)
    low = (entries - high.astype(F32)).astype(BF16)
    lane, part = iota((2 * slots, rows), 1).astype(F32), iota((2 * slots, rows), 0) % 2
    for b in range(blocks):
        spot = lane == blocks * pick_ref[...] + b
        picked = jnp.dot((spot & (part == 0)).astype(BF16), high, preferred_element_type=F32)
        if both:
            picked = picked + jnp.dot((spot & (part == 1)).astype(BF16), low, preferred_element_type=F32)
        picked_ref[:, b * LANES : (b + 1) * LANES] = picked
    for t in range(slots):
        if tile_copies and t % (slots // CHUNKS) == 0:
            tile_copies[t // (slots // CHUNKS)].wait()
        product_ref[2 * t : 2 * t + 2] = lax.dot_general(
            picked_ref[2 * t : 2 * t + 2].astype(BF16),
            tiles_ref[t],
            (((1,), (1 if forward else 0,)), ((), ())),
            preferred_element_type=F32,
        )
    sub = iota((rows, 2 * slots), 0).astype(F32)
    out = None
    for b in range(blocks):
        hot = (sub == blocks * put_ref[...] + b).astype(F32)
        part = jnp.dot(
            hot, product_ref[:, b * LANES : (b + 1) * LANES], precision=HIGH, preferred_element_type=F32
        )
        out = part if out is None else out + part
    return out


def first_forward_kernel(
    got_ref, tiles_hbm, pick_ref, put_ref, gram_ref, message_ref, picked_ref, product_ref, tile_sems, tiles_ref
):
    copies = started(tiles_hbm, tiles_ref, tile_sems)
    entries = got_ref[...].reshape(-1, LANES)
    sums = multiplied(True, False, entries, tiles_ref, copies, pick_ref, put_ref, picked_ref, product_ref).astype(BF16)
    rows = sums.shape[0]
    gram = gram_ref[...]
    high = gram.astype(BF16).astype(F32)
    middle = (gram - high).astype(BF16).astype(F32)
    low = gram - high - middle
    first = jnp.concatenate([high, middle], axis=0).astype(BF16)
    second = jnp.concatenate([low, jnp.zeros_like(low)], axis=0).astype(BF16)
    for k in range(message_ref.shape[0]):
        message_ref[k, :rows] = sums
        message_ref[k, rows : rows + 16] = first
        message_ref[k, rows + 16 : rows + 32] = second


def forward_kernel(got_ref, tiles_ref, pick_ref, put_ref, message_ref, picked_ref, product_ref):
    entries = got_ref[...].reshape(-1, LANES)
    sums = multiplied(True, True, entries, tiles_ref, [], pick_ref, put_ref, picked_ref, product_ref)
    message_ref[...] = jnp.broadcast_to(sums.astype(BF16)[None], message_ref.shape)


def dots_kernel(length, first, own_ref, got_ref, *refs):
    if first:
        *pairs, image_ref, message_ref, near_ref, sems = refs
        others = []
        ranks = [own_ref[0] ^ (PLACES * h + k) for k in range(PLACES) for h in range(2)]
        copies = [
            pltpu.make_async_copy(pairs[n // 2].at[n % 2], near_ref.at[rank], sems.at[n])
            for n, rank in enumerate(ranks)
        ]
        for copy in copies:
            copy.start()
    else:
        near_ref, *others, image_ref, message_ref = refs
        ranks, copies = range(near_ref.shape[0]), []
    image = jnp.sum(got_ref[:, :LANES].astype(F32), axis=0)
    image_ref[...] = image
    _, count, width = near_ref.shape
    across = width // LANES
    acc = jnp.zeros((count, LANES), F32)
    for n, rank in enumerate(ranks):
        if copies:
            copies[n].wait()
        start = rank * across
        part = image_ref[pl.ds(pl.multiple_of(start, across) if first else start, across)]
        for j in range(across):
            acc = acc + near_ref[rank, :, j * LANES : (j + 1) * LANES] * part[j : j + 1]
    dots = padded(jnp.sum(acc, axis=1, keepdims=True))
    for n, other in enumerate(others):
        dots = dots + at(total(other[...].reshape(image.shape) * image), count + n)
    dots = dots + at(total(image * image), PAD - 1)
    row = as_row(dots) * (1.0 / length)
    if first:
        grams = jnp.sum(got_ref[:, LANES:].astype(F32), axis=0)
        gram = (grams[:8] + grams[8:16] + grams[16:24]) * (1.0 / length)
        message_ref[:, :8] = jnp.broadcast_to(gram[None], (message_ref.shape[0], 8, LANES))
        message_ref[:, 8:] = jnp.broadcast_to(row[None], (message_ref.shape[0], 8, LANES))
    else:
        message_ref[...] = jnp.broadcast_to(row, message_ref.shape)


def split_dots(row):
    col = as_col(row)
    last = iota((PAD, 1), 0) == PAD - 1
    return jnp.where(last, 0.0, col), total(jnp.where(last, col, 0.0))


def vector_kernel(
    m, known, own_ref, got_ref, image_ref, wide_ref, tiles_ref, pick_ref, put_ref, *refs
):
    copies = []
    if known:
        *refs, picked_ref, product_ref = refs
    else:
        *refs, near_ref, picked_ref, product_ref, tile_sems = refs
        copies = started(tiles_ref, near_ref, tile_sems)
        tiles_ref = near_ref
    *inputs, new_ref, own_out_ref, gram_ref, scale_ref, message_ref = refs
    parts, count, width = wide_ref.shape
    if known:
        gram = inputs[0][...]
        row = jnp.sum(got_ref[...], axis=0, keepdims=True)
        others = inputs[1:]
    else:
        got = jnp.sum(got_ref[...], axis=0)
        gram = unpacked(got[:8], count + 1)
        row = got[8:9]
        others = inputs
    dots, square = split_dots(row)
    coef, scale, inverse, grown = solve(gram, dots, square, m)
    gram_ref[...] = grown
    scale_ref[...] = jnp.broadcast_to(scale, scale_ref.shape)
    across = width // LANES
    by_lane = jnp.broadcast_to(coef[:count], (count, LANES))
    for k in range(parts):
        sums = [
            jnp.sum(wide_ref[k, :, j * LANES : (j + 1) * LANES] * by_lane, axis=0, keepdims=True)
            for j in range(across)
        ]
        span = slice(k * across, (k + 1) * across)
        new_ref[span] = image_ref[span] - jnp.concatenate(sums, axis=0)
    new = new_ref[...]
    for n, other in enumerate(others):
        new = new - coef[count + n : count + n + 1] * other[...].reshape(new.shape)
    new = new * inverse
    new_ref[...] = new
    own_out_ref[...] = new_ref[pl.ds(pl.multiple_of(own_ref[0] * across, across), across)]
    sums = multiplied(False, True, new, tiles_ref, copies, pick_ref, put_ref, picked_ref, product_ref)
    message_ref[...] = sums.reshape(message_ref.shape)


def right_dots_kernel(length, got_ref, basis_ref, *refs):
    refs = list(refs)
    image_ref, message_ref = refs[-2:]
    others = refs[:-2]
    image = jnp.sum(got_ref[...], axis=0)
    image_ref[...] = image
    count = basis_ref.shape[0]
    acc = jnp.zeros((count, LANES), F32)
    for j in range(image.shape[0]):
        acc = acc + basis_ref[:, j * LANES : (j + 1) * LANES] * image_ref[j : j + 1]
    dots = padded(jnp.sum(acc, axis=1, keepdims=True))
    for n, other in enumerate(others):
        dots = dots + at(total(other[...] * image), count + n)
    dots = dots + at(total(image * image), PAD - 1)
    message_ref[...] = jnp.broadcast_to(as_row(dots) * (1.0 / length), message_ref.shape)


def new_right(m, got_ref, image_ref, basis_ref, gram_ref, others):
    count = basis_ref.shape[0]
    dots, square = split_dots(jnp.sum(got_ref[...], axis=0, keepdims=True))
    coef, scale, inverse, grown = solve(gram_ref[...], dots, square, m)
    new = projected_slice(image_ref, basis_ref, coef)
    for n, other in enumerate(others):
        new = new - coef[count + n : count + n + 1] * other[...]
    return new * inverse, scale, grown


def right_kernel(m, got_ref, image_ref, basis_ref, gram_in_ref, *refs):
    refs = list(refs)
    vector_ref, gram_ref, scale_ref, message_ref = refs[-4:]
    new, scale, grown = new_right(m, got_ref, image_ref, basis_ref, gram_in_ref, refs[:-4])
    vector_ref[...] = new
    gram_ref[...] = grown
    scale_ref[...] = jnp.broadcast_to(scale, scale_ref.shape)
    message_ref[...] = jnp.broadcast_to(new[None], message_ref.shape)


def put_rows(out_ref, row, vector):
    for j in range(vector.shape[0]):
        out_ref[row : row + 1, j * LANES : (j + 1) * LANES] = vector[j : j + 1]


def last_kernel(
    m, got_ref, image_ref, basis_ref, gram_ref, old_0_ref, old_1_ref,
    alpha_0_ref, alpha_1_ref, beta_0_ref, out_ref, scales_ref,
):
    new, scale, _ = new_right(m, got_ref, image_ref, basis_ref, gram_ref, [old_0_ref, old_1_ref])
    count = basis_ref.shape[0]
    out_ref[:count] = basis_ref[...]
    put_rows(out_ref, count, old_0_ref[...])
    put_rows(out_ref, count + 1, old_1_ref[...])
    put_rows(out_ref, count + 2, new)
    lane = iota((1, LANES), 1)
    alphas = jnp.where(lane == 0, alpha_0_ref[...], alpha_1_ref[...])
    betas = jnp.where(lane == 0, beta_0_ref[...], jnp.broadcast_to(scale, (1, LANES)))
    scales_ref[...] = jnp.concatenate([alphas, betas], axis=0)[:, :2]


def left_out_kernel(basis_ref, new_0_ref, new_1_ref, out_ref):
    count = basis_ref.shape[0]
    out_ref[:count] = basis_ref[...]
    put_rows(out_ref, count, new_0_ref[...])
    put_rows(out_ref, count + 1, new_1_ref[...])


WHOLE = pl.BlockSpec(memory_space=pltpu.VMEM)
SCALAR = pl.BlockSpec(memory_space=pltpu.SMEM)
ANYWHERE = pl.BlockSpec(memory_space=pl.ANY)
FAR = pl.BlockSpec(memory_space=pltpu.HBM)


def turned(x, axis, count, k):
    return lax.ppermute(x, axis, [(i, i ^ k) for i in range(count)])


def in_hbm(x):
    return pltpu.with_memory_space_constraint(x, pltpu.HBM)


def in_vmem(x):
    return pltpu.with_memory_space_constraint(x, pltpu.VMEM)


def call(kernel, name, outs, args, scalars=(), scratch=(), far=(), near=(), any_place=()):
    shapes = tuple(jax.ShapeDtypeStruct(s, F32) if isinstance(s, tuple) else s for s in outs)
    specs = [
        SCALAR if i in scalars else FAR if i in far else ANYWHERE if i in any_place else WHOLE
        for i in range(len(args))
    ]
    return pl.pallas_call(
        kernel,
        name=name,
        out_shape=shapes,
        in_specs=specs,
        out_specs=tuple(WHOLE for _ in shapes),
        scratch_shapes=list(scratch),
        compiler_params=pltpu.CompilerParams(vmem_limit_bytes=VMEM_LIMIT),
    )(*(in_hbm(x) if i in far else in_vmem(x) if i in near else x for i, x in enumerate(args)))


def after(x, *earlier):
    return lax.optimization_barrier((x, *earlier))[0]


def per_device(
    u_start, v_start, keep_u, keep_v, v_next, tile_blocks, tile_rows, tile_cols, tile_count
):
    rows_n, cols_n = lax.axis_size(ROW), lax.axis_size(COL)
    devices = rows_n * cols_n
    keep = keep_u.shape[1]
    slots, size = tile_blocks.shape[:2]
    u_here, u_range = u_start.shape
    v_here, v_range = v_start.shape
    u_own, v_own = u_range // cols_n, v_range // rows_n
    u_length, v_length = u_range * rows_n, v_range * cols_n
    u_rows, v_rows = u_own // LANES, v_own // LANES
    u_full, v_full = u_range // LANES, v_range // LANES
    products = [pltpu.VMEM((2 * slots, size), F32), pltpu.VMEM((2 * slots, size), F32)]
    sems = [pltpu.SemaphoreType.DMA((CHUNKS,))]
    narrow = functools.partial(jax.ShapeDtypeStruct, dtype=BF16)

    own_u = lax.axis_index(COL).reshape(1)
    u_blocks, keep_u, keep_v, next_rows, row_lane, col_lane, row_sub, col_sub = call(
        prepare_kernel,
        "prepare",
        [
            (cols_n, u_here, u_own),
            keep_u.T.shape,
            keep_v.T.shape,
            (v_rows, LANES),
            (1, 2 * slots),
            (1, 2 * slots),
            (2 * slots, 1),
            (2 * slots, 1),
        ],
        [
            tile_count,
            own_u,
            u_start,
            tile_rows.reshape(1, slots),
            tile_cols.reshape(1, slots),
            keep_u.T,
            keep_v.T,
            v_next.reshape(v_rows, LANES),
        ],
        scalars=(0, 1),
        scratch=[pltpu.VMEM((2, 1, slots), jnp.int32), pltpu.SemaphoreType.DMA((cols_n + 5,))],
        far=range(2, 8),
    )
    u_got = swapped(u_blocks, COL).reshape(-1, u_own)
    u_kept, u_gram = call(kept_kernel, "left_kept", [(keep, u_own), (8, LANES)], [u_got, keep_u])
    u_sent = u_kept.astype(jnp.float16)
    u_came = turned(u_sent, COL[0], 2, 1)

    v_blocks = after(jnp.moveaxis(v_start.reshape(v_here, rows_n, v_own), 1, 0), u_kept)
    v_got, u_came = lax.optimization_barrier((swapped(v_blocks, ROW).reshape(-1, v_own), u_came))
    u_pair = jnp.stack([u_sent, u_came])
    u_pairs = [u_pair] + [turned(u_pair, COL[1], PLACES, k) for k in range(1, PLACES)]
    v_kept, message = call(
        kept_with_kernel,
        "right_kept",
        [(keep, v_own), (devices, 8, LANES)],
        [after(v_got, u_pair), keep_v, next_rows],
        scratch=[pltpu.VMEM((LANES, v_own), F32)],
    )
    got = swapped(message, ROW_COL)
    v_0, gram_v, message = call(
        functools.partial(first_kernel, v_length),
        "first_right",
        [(v_rows, LANES), (PAD, LANES), (rows_n, v_rows, LANES)],
        [got, v_kept, next_rows],
    )
    tile_room = [pltpu.VMEM(tile_blocks.shape, BF16)]
    (message,) = call(
        first_forward_kernel,
        "forward",
        [narrow((cols_n, u_full + 32, LANES))],
        [swapped(message, ROW), tile_blocks, col_sub, row_lane, u_gram],
        scratch=products + sems + tile_room,
        far=(1,),
    )
    got = swapped(message, COL)
    image, dots, u_near = call(
        functools.partial(dots_kernel, u_length, True),
        "left_dots",
        [(u_full, LANES), (rows_n, 16, LANES), pltpu.VMEM((cols_n, keep, u_own), F32)],
        [own_u, got, *(pair.astype(F32) for pair in u_pairs)],
        scalars=(0,),
        scratch=sems,
        any_place=range(2, 2 + PLACES),
    )

    def left(dots, image, tiles, m, gram, others):
        known = [] if gram is None else [gram]
        keep_tiles = [] if known else tile_room
        return call(
            functools.partial(vector_kernel, m, bool(known)),
            "left",
            [(u_full, LANES), (u_rows, LANES), (PAD, LANES), (1, LANES), (rows_n, v_rows, LANES), *keep_tiles],
            [own_u, swapped(dots, ROW), image, u_near, tiles, row_sub, col_lane, *known, *others],
            scalars=(0,),
            scratch=products if known else products + sems,
            near=(3, 4) if known else (3,),
            far=() if known else (4,),
        )

    u_0_wide, u_0, gram_u, alpha_0, message, tiles = left(dots, image, tile_blocks, keep, None, [])
    image, dots = call(
        functools.partial(right_dots_kernel, v_length),
        "right_dots",
        [(v_rows, LANES), (devices, LANES)],
        [swapped(message, ROW), v_kept, v_0],
    )
    v_1, gram_v, beta_0, message = call(
        functools.partial(right_kernel, keep + 1),
        "right",
        [(v_rows, LANES), (PAD, LANES), (1, LANES), (rows_n, v_rows, LANES)],
        [swapped(dots, ROW_COL), image, v_kept, gram_v, v_0],
    )
    (message,) = call(
        forward_kernel,
        "forward",
        [narrow((cols_n, u_full, LANES))],
        [swapped(message, ROW), tiles, col_sub, row_lane],
        scratch=products,
        near=(1,),
    )
    image, dots = call(
        functools.partial(dots_kernel, u_length, False),
        "left_dots",
        [(u_full, LANES), (rows_n, LANES)],
        [own_u, swapped(message, COL), u_near, u_0_wide],
        scalars=(0,),
        near=(2,),
    )
    _, u_1, _, alpha_1, message = left(dots, image, tiles, keep + 1, gram_u, [u_0_wide])
    got = swapped(message, ROW)
    (u_basis,) = call(left_out_kernel, "left_out", [(keep + 2, u_own)], [u_kept, u_0, u_1])
    image, dots = call(
        functools.partial(right_dots_kernel, v_length),
        "last_dots",
        [(v_rows, LANES), (devices, LANES)],
        [got, v_kept, v_0, v_1],
    )
    v_basis, scales = call(
        functools.partial(last_kernel, keep + 2),
        "last_right",
        [(keep + 3, v_own), (2, 2)],
        [swapped(dots, ROW_COL), image, v_kept, gram_v, v_0, v_1, alpha_0, alpha_1, beta_0],
    )
    return u_basis, v_basis, scales


def solution(mesh):
    finer = Mesh(mesh.devices.reshape(2, 4, 2, 2, 4), ROW_COL)
    return jax.shard_map(
        per_device,
        mesh=finer,
        in_specs=(
            P(COL, ROW),
            P(ROW, COL),
            P(),
            P(),
            P(COL_ROW),
            P(ROW_COL, None, None),
            P(ROW_COL),
            P(ROW_COL),
            P(ROW_COL),
        ),
        out_specs=(P(None, ROW_COL), P(None, COL_ROW), P()),
        check_vma=False,
    )
```

```python
import functools

import jax
import jax.numpy as jnp
from jax import lax
from jax.experimental import pallas as pl
from jax.experimental.pallas import tpu as pltpu
from jax.sharding import Mesh
from jax.sharding import PartitionSpec as P

ROW = ("row_0", "row_1", "row_2")
COL = ("col_0", "col_1")
ROW_COL = ROW + COL
COL_ROW = COL + ROW

HIGH = lax.Precision.HIGHEST
F32 = jnp.float32
BF16 = jnp.bfloat16
LANES = 128
PAD = 48
PLACES = 4
EPS = 1e-06
VMEM_LIMIT = 24 << 20
CHUNKS = 8


def swapped(blocks, axis):
    return lax.all_to_all(blocks, axis, 0, 0, tiled=True)


def iota(shape, dim):
    return lax.broadcasted_iota(jnp.int32, shape, dim)


def as_row(col):
    spot = iota((PAD, LANES), 0) == iota((PAD, LANES), 1)
    return jnp.sum(jnp.where(spot, col, 0.0), axis=0, keepdims=True)


def as_col(row):
    spot = iota((PAD, LANES), 0) == iota((PAD, LANES), 1)
    return jnp.sum(jnp.where(spot, row, 0.0), axis=1, keepdims=True)


def total(x):
    return jnp.sum(jnp.sum(x, axis=1, keepdims=True), axis=0, keepdims=True)


def packed(gram, n):
    width = n // 2 + 1
    twice = gram + pltpu.roll(gram, n, 1)
    turned, sub = twice, iota((PAD, LANES), 0)
    for bit in (1, 2, 4, 8, 16, 32):
        turned = jnp.where(sub & bit != 0, pltpu.roll(turned, LANES - bit, 1), turned)
    turned = jnp.where(iota((PAD, LANES), 1) < width, turned, 0.0)
    out = turned[0:8]
    for g in range(1, PAD // 8):
        out = out + pltpu.roll(turned[8 * g : 8 * g + 8], width * g, 1)
    return out


def unpacked(pack, n):
    width = n // 2 + 1
    groups = [pack] + [
        pltpu.roll(pack, LANES - width * g, 1) for g in range(1, PAD // 8)
    ]
    turned = jnp.concatenate(groups, axis=0)
    turned = jnp.where(iota((PAD, LANES), 1) < width, turned, 0.0)
    wide = pltpu.roll(turned, 0, 1, stride=1, stride_axis=0)
    half = wide + pltpu.roll(wide, LANES - n, 1)
    lane, sub = iota((PAD, LANES), 1), iota((PAD, LANES), 0)
    half = jnp.where((lane < n) & (sub < n), half, 0.0)
    square = jnp.concatenate([half, jnp.zeros((LANES - PAD, LANES), F32)], axis=0)
    return half + jnp.where(lane == sub, 0.0, square.T[:PAD])


def solve(gram, dots_col, square, m):
    coef_col = 2.0 * dots_col - jnp.sum(gram * as_row(dots_col), axis=1, keepdims=True)
    across = dots_col - jnp.sum(gram * as_row(coef_col), axis=1, keepdims=True)
    mean_square = square - total(coef_col * (dots_col + across))
    mean_square = jnp.maximum(mean_square, 0.0)
    scale = jnp.sqrt(mean_square + EPS)
    inverse = 1.0 / scale
    across = across * inverse
    lane, sub = iota((PAD, LANES), 1), iota((PAD, LANES), 0)
    grown = jnp.where(sub == m, as_row(across), gram)
    grown = jnp.where(lane == m, across, grown)
    grown = jnp.where((lane == m) & (sub == m), mean_square * inverse * inverse, grown)
    return coef_col, scale, inverse, grown


def at(value, index):
    return jnp.where(iota((PAD, 1), 0) == index, value, 0.0)


def padded(col):
    return jnp.concatenate([col, jnp.zeros((PAD - col.shape[0], 1), F32)], axis=0)


def prepare_kernel(
    count_ref, own_ref, start_ref, rows_ref, cols_ref, keep_u_ref, keep_v_ref, next_ref,
    out_ref, keep_u_out, keep_v_out, next_out, row_lane_ref, col_lane_ref, row_sub_ref, col_sub_ref,
    index_ref, sems,
):
    blocks, _, width = out_ref.shape
    pairs = [(start_ref.at[:, k * width : (k + 1) * width], out_ref.at[k]) for k in range(blocks)]
    pairs += [(keep_u_ref, keep_u_out), (keep_v_ref, keep_v_out), (next_ref, next_out)]
    pairs += [(rows_ref, index_ref.at[0]), (cols_ref, index_ref.at[1])]
    copies = [pltpu.make_async_copy(a, b, sems.at[n]) for n, (a, b) in enumerate(pairs)]
    for copy in copies:
        copy.start()
    for copy in copies[::-1]:
        copy.wait()
    slots = rows_ref.shape[1]
    double = 2 * slots
    pair = iota((double, slots), 0) // 2 == iota((double, slots), 1)
    spot = iota((double, double), 0) == iota((double, double), 1)
    used = iota((1, double), 1) // 2 < count_ref[0]
    for n, (lane_ref, sub_ref) in enumerate(((row_lane_ref, row_sub_ref), (col_lane_ref, col_sub_ref))):
        sub = jnp.sum(jnp.where(pair, index_ref[n].astype(F32), 0.0), axis=1, keepdims=True)
        sub_ref[...] = sub
        lane = jnp.sum(jnp.where(spot, sub, 0.0), axis=0, keepdims=True)
        lane_ref[...] = jnp.where(used, lane, -1.0)


def kept_kernel(start_ref, keep_ref, out_ref):
    out_ref[...] = jnp.dot(keep_ref[...], start_ref[...], precision=HIGH, preferred_element_type=F32)


def gram_kernel(basis_ref, gram_ref):
    basis = basis_ref[...]
    rows, width = basis.shape
    wide = jnp.concatenate([basis, jnp.zeros((PAD - rows, width), F32)], axis=0)
    full = jnp.concatenate([wide, jnp.zeros((LANES - PAD, width), F32)], axis=0)
    gram = lax.dot_general(
        wide, full, (((1,), (1,)), ((), ())), precision=HIGH, preferred_element_type=F32
    )
    gram_ref[...] = packed(gram, rows + 1)


def kept_with_kernel(start_ref, keep_ref, next_ref, out_ref, message_ref, wide_ref):
    basis = jnp.dot(keep_ref[...], start_ref[...], precision=HIGH, preferred_element_type=F32)
    out_ref[...] = basis
    rows = basis.shape[0]
    wide_ref[...] = jnp.zeros_like(wide_ref)
    wide_ref[:rows] = basis
    for j in range(next_ref.shape[0]):
        wide_ref[rows : rows + 1, j * LANES : (j + 1) * LANES] = next_ref[j : j + 1]
    full = wide_ref[...]
    gram = lax.dot_general(
        full[:PAD], full, (((1,), (1,)), ((), ())), precision=HIGH, preferred_element_type=F32
    )
    message_ref[...] = jnp.broadcast_to(packed(gram, rows + 1)[None], message_ref.shape)


def projected_slice(vector_ref, basis_ref, coef_col):
    count = basis_ref.shape[0]
    rows = []
    for j in range(vector_ref.shape[0]):
        part = basis_ref[:, j * LANES : (j + 1) * LANES] * coef_col[:count]
        rows.append(jnp.sum(part, axis=0, keepdims=True))
    return vector_ref[...] - jnp.concatenate(rows, axis=0)


def first_kernel(length, got_ref, basis_ref, next_ref, vector_ref, gram_ref, message_ref):
    count = basis_ref.shape[0]
    gram = unpacked(jnp.sum(got_ref[...], axis=0), count + 1) * (1.0 / length)
    lane, sub = iota((PAD, LANES), 1), iota((PAD, LANES), 0)
    dots = jnp.sum(jnp.where((lane == count) & (sub < count), gram, 0.0), axis=1, keepdims=True)
    square = total(jnp.where((lane == count) & (sub == count), gram, 0.0))
    gram = jnp.where((lane < count) & (sub < count), gram, 0.0)
    coef, scale, inverse, grown = solve(gram, dots, square, count)
    new = projected_slice(next_ref, basis_ref, coef) * inverse
    vector_ref[...] = new
    gram_ref[...] = grown
    message_ref[...] = jnp.broadcast_to(new[None], message_ref.shape)


def started(source, target, sems):
    parts = sems.shape[0]
    step = source.shape[0] // parts
    copies = [
        pltpu.make_async_copy(
            source.at[n * step : (n + 1) * step], target.at[n * step : (n + 1) * step], sems.at[n]
        )
        for n in range(parts)
    ]
    for copy in copies:
        copy.start()
    return copies


def multiplied(forward, both, entries, tiles_ref, tile_copies, pick_ref, put_ref, picked_ref, product_ref):
    slots, size = tiles_ref.shape[:2]
    blocks = size // LANES
    rows = entries.shape[0]
    high = entries.astype(BF16)
    low = (entries - high.astype(F32)).astype(BF16)
    lane, part = iota((2 * slots, rows), 1).astype(F32), iota((2 * slots, rows), 0) % 2
    for b in range(blocks):
        spot = lane == blocks * pick_ref[...] + b
        picked = jnp.dot((spot & (part == 0)).astype(BF16), high, preferred_element_type=F32)
        if both:
            picked = picked + jnp.dot((spot & (part == 1)).astype(BF16), low, preferred_element_type=F32)
        picked_ref[:, b * LANES : (b + 1) * LANES] = picked
    for t in range(slots):
        if tile_copies and t % (slots // CHUNKS) == 0:
            tile_copies[t // (slots // CHUNKS)].wait()
        product_ref[2 * t : 2 * t + 2] = lax.dot_general(
            picked_ref[2 * t : 2 * t + 2].astype(BF16),
            tiles_ref[t],
            (((1,), (1 if forward else 0,)), ((), ())),
            preferred_element_type=F32,
        )
    sub = iota((rows, 2 * slots), 0).astype(F32)
    out = None
    for b in range(blocks):
        hot = (sub == blocks * put_ref[...] + b).astype(F32)
        part = jnp.dot(
            hot, product_ref[:, b * LANES : (b + 1) * LANES], precision=HIGH, preferred_element_type=F32
        )
        out = part if out is None else out + part
    return out


def first_forward_kernel(
    got_ref, tiles_hbm, pick_ref, put_ref, gram_ref, message_ref, picked_ref, product_ref, tile_sems, tiles_ref
):
    copies = started(tiles_hbm, tiles_ref, tile_sems)
    entries = got_ref[...].reshape(-1, LANES)
    sums = multiplied(True, False, entries, tiles_ref, copies, pick_ref, put_ref, picked_ref, product_ref).astype(BF16)
    rows = sums.shape[0]
    gram = gram_ref[...]
    high = gram.astype(BF16).astype(F32)
    middle = (gram - high).astype(BF16).astype(F32)
    low = gram - high - middle
    first = jnp.concatenate([high, middle], axis=0).astype(BF16)
    second = jnp.concatenate([low, jnp.zeros_like(low)], axis=0).astype(BF16)
    for k in range(message_ref.shape[0]):
        message_ref[k, :rows] = sums
        message_ref[k, rows : rows + 16] = first
        message_ref[k, rows + 16 : rows + 32] = second


def forward_kernel(got_ref, tiles_ref, pick_ref, put_ref, message_ref, picked_ref, product_ref):
    entries = got_ref[...].reshape(-1, LANES)
    sums = multiplied(True, True, entries, tiles_ref, [], pick_ref, put_ref, picked_ref, product_ref)
    message_ref[...] = jnp.broadcast_to(sums.astype(BF16)[None], message_ref.shape)


def dots_kernel(length, first, own_ref, got_ref, *refs):
    if first:
        *pairs, image_ref, message_ref, near_ref, sems = refs
        others = []
        ranks = [own_ref[0] ^ (PLACES * h + k) for k in range(PLACES) for h in range(2)]
        copies = [
            pltpu.make_async_copy(pairs[n // 2].at[n % 2], near_ref.at[rank], sems.at[n])
            for n, rank in enumerate(ranks)
        ]
        for copy in copies:
            copy.start()
    else:
        near_ref, *others, image_ref, message_ref = refs
        ranks, copies = range(near_ref.shape[0]), []
    image = jnp.sum(got_ref[:, :LANES].astype(F32), axis=0)
    image_ref[...] = image
    _, count, width = near_ref.shape
    across = width // LANES
    acc = jnp.zeros((count, LANES), F32)
    for n, rank in enumerate(ranks):
        if copies:
            copies[n].wait()
        start = rank * across
        part = image_ref[pl.ds(pl.multiple_of(start, across) if first else start, across)]
        for j in range(across):
            acc = acc + near_ref[rank, :, j * LANES : (j + 1) * LANES] * part[j : j + 1]
    dots = padded(jnp.sum(acc, axis=1, keepdims=True))
    for n, other in enumerate(others):
        dots = dots + at(total(other[...].reshape(image.shape) * image), count + n)
    dots = dots + at(total(image * image), PAD - 1)
    row = as_row(dots) * (1.0 / length)
    if first:
        grams = jnp.sum(got_ref[:, LANES:].astype(F32), axis=0)
        gram = (grams[:8] + grams[8:16] + grams[16:24]) * (1.0 / length)
        message_ref[:, :8] = jnp.broadcast_to(gram[None], (message_ref.shape[0], 8, LANES))
        message_ref[:, 8:] = jnp.broadcast_to(row[None], (message_ref.shape[0], 8, LANES))
    else:
        message_ref[...] = jnp.broadcast_to(row, message_ref.shape)


def split_dots(row):
    col = as_col(row)
    last = iota((PAD, 1), 0) == PAD - 1
    return jnp.where(last, 0.0, col), total(jnp.where(last, col, 0.0))


def vector_kernel(
    m, known, own_ref, got_ref, image_ref, wide_ref, tiles_ref, pick_ref, put_ref, *refs
):
    copies = []
    if known:
        *refs, picked_ref, product_ref = refs
    else:
        *refs, near_ref, picked_ref, product_ref, tile_sems = refs
        copies = started(tiles_ref, near_ref, tile_sems)
        tiles_ref = near_ref
    *inputs, new_ref, own_out_ref, gram_ref, scale_ref, message_ref = refs
    parts, count, width = wide_ref.shape
    if known:
        gram = inputs[0][...]
        row = jnp.sum(got_ref[...], axis=0, keepdims=True)
        others = inputs[1:]
    else:
        got = jnp.sum(got_ref[...], axis=0)
        gram = unpacked(got[:8], count + 1)
        row = got[8:9]
        others = inputs
    dots, square = split_dots(row)
    coef, scale, inverse, grown = solve(gram, dots, square, m)
    gram_ref[...] = grown
    scale_ref[...] = jnp.broadcast_to(scale, scale_ref.shape)
    across = width // LANES
    by_lane = jnp.broadcast_to(coef[:count], (count, LANES))
    for k in range(parts):
        sums = [
            jnp.sum(wide_ref[k, :, j * LANES : (j + 1) * LANES] * by_lane, axis=0, keepdims=True)
            for j in range(across)
        ]
        span = slice(k * across, (k + 1) * across)
        new_ref[span] = image_ref[span] - jnp.concatenate(sums, axis=0)
    new = new_ref[...]
    for n, other in enumerate(others):
        new = new - coef[count + n : count + n + 1] * other[...].reshape(new.shape)
    new = new * inverse
    new_ref[...] = new
    own_out_ref[...] = new_ref[pl.ds(pl.multiple_of(own_ref[0] * across, across), across)]
    sums = multiplied(False, True, new, tiles_ref, copies, pick_ref, put_ref, picked_ref, product_ref)
    message_ref[...] = sums.reshape(message_ref.shape)


def right_dots_kernel(length, got_ref, basis_ref, *refs):
    refs = list(refs)
    image_ref, message_ref = refs[-2:]
    others = refs[:-2]
    image = jnp.sum(got_ref[...], axis=0)
    image_ref[...] = image
    count = basis_ref.shape[0]
    acc = jnp.zeros((count, LANES), F32)
    for j in range(image.shape[0]):
        acc = acc + basis_ref[:, j * LANES : (j + 1) * LANES] * image_ref[j : j + 1]
    dots = padded(jnp.sum(acc, axis=1, keepdims=True))
    for n, other in enumerate(others):
        dots = dots + at(total(other[...] * image), count + n)
    dots = dots + at(total(image * image), PAD - 1)
    message_ref[...] = jnp.broadcast_to(as_row(dots) * (1.0 / length), message_ref.shape)


def new_right(m, got_ref, image_ref, basis_ref, gram_ref, others):
    count = basis_ref.shape[0]
    dots, square = split_dots(jnp.sum(got_ref[...], axis=0, keepdims=True))
    coef, scale, inverse, grown = solve(gram_ref[...], dots, square, m)
    new = projected_slice(image_ref, basis_ref, coef)
    for n, other in enumerate(others):
        new = new - coef[count + n : count + n + 1] * other[...]
    return new * inverse, scale, grown


def right_kernel(m, got_ref, image_ref, basis_ref, gram_in_ref, *refs):
    refs = list(refs)
    vector_ref, gram_ref, scale_ref, message_ref = refs[-4:]
    new, scale, grown = new_right(m, got_ref, image_ref, basis_ref, gram_in_ref, refs[:-4])
    vector_ref[...] = new
    gram_ref[...] = grown
    scale_ref[...] = jnp.broadcast_to(scale, scale_ref.shape)
    message_ref[...] = jnp.broadcast_to(new[None], message_ref.shape)


def put_rows(out_ref, row, vector):
    for j in range(vector.shape[0]):
        out_ref[row : row + 1, j * LANES : (j + 1) * LANES] = vector[j : j + 1]


def last_kernel(
    m, got_ref, image_ref, basis_ref, gram_ref, old_0_ref, old_1_ref,
    alpha_0_ref, alpha_1_ref, beta_0_ref, out_ref, scales_ref,
):
    new, scale, _ = new_right(m, got_ref, image_ref, basis_ref, gram_ref, [old_0_ref, old_1_ref])
    count = basis_ref.shape[0]
    out_ref[:count] = basis_ref[...]
    put_rows(out_ref, count, old_0_ref[...])
    put_rows(out_ref, count + 1, old_1_ref[...])
    put_rows(out_ref, count + 2, new)
    lane = iota((1, LANES), 1)
    alphas = jnp.where(lane == 0, alpha_0_ref[...], alpha_1_ref[...])
    betas = jnp.where(lane == 0, beta_0_ref[...], jnp.broadcast_to(scale, (1, LANES)))
    scales_ref[...] = jnp.concatenate([alphas, betas], axis=0)[:, :2]


def left_out_kernel(basis_ref, new_0_ref, new_1_ref, out_ref):
    count = basis_ref.shape[0]
    out_ref[:count] = basis_ref[...]
    put_rows(out_ref, count, new_0_ref[...])
    put_rows(out_ref, count + 1, new_1_ref[...])


WHOLE = pl.BlockSpec(memory_space=pltpu.VMEM)
SCALAR = pl.BlockSpec(memory_space=pltpu.SMEM)
ANYWHERE = pl.BlockSpec(memory_space=pl.ANY)
FAR = pl.BlockSpec(memory_space=pltpu.HBM)


def turned(x, axis, count, k):
    return lax.ppermute(x, axis, [(i, i ^ k) for i in range(count)])


def in_hbm(x):
    return pltpu.with_memory_space_constraint(x, pltpu.HBM)


def in_vmem(x):
    return pltpu.with_memory_space_constraint(x, pltpu.VMEM)


def call(kernel, name, outs, args, scalars=(), scratch=(), far=(), near=(), any_place=()):
    shapes = tuple(jax.ShapeDtypeStruct(s, F32) if isinstance(s, tuple) else s for s in outs)
    specs = [
        SCALAR if i in scalars else FAR if i in far else ANYWHERE if i in any_place else WHOLE
        for i in range(len(args))
    ]
    return pl.pallas_call(
        kernel,
        name=name,
        out_shape=shapes,
        in_specs=specs,
        out_specs=tuple(WHOLE for _ in shapes),
        scratch_shapes=list(scratch),
        compiler_params=pltpu.CompilerParams(vmem_limit_bytes=VMEM_LIMIT),
    )(*(in_hbm(x) if i in far else in_vmem(x) if i in near else x for i, x in enumerate(args)))


def after(x, *earlier):
    return lax.optimization_barrier((x, *earlier))[0]


def per_device(
    u_start, v_start, keep_u, keep_v, v_next, tile_blocks, tile_rows, tile_cols, tile_count
):
    rows_n, cols_n = lax.axis_size(ROW), lax.axis_size(COL)
    devices = rows_n * cols_n
    keep = keep_u.shape[1]
    slots, size = tile_blocks.shape[:2]
    u_here, u_range = u_start.shape
    v_here, v_range = v_start.shape
    u_own, v_own = u_range // cols_n, v_range // rows_n
    u_length, v_length = u_range * rows_n, v_range * cols_n
    u_rows, v_rows = u_own // LANES, v_own // LANES
    u_full, v_full = u_range // LANES, v_range // LANES
    products = [pltpu.VMEM((2 * slots, size), F32), pltpu.VMEM((2 * slots, size), F32)]
    sems = [pltpu.SemaphoreType.DMA((CHUNKS,))]
    narrow = functools.partial(jax.ShapeDtypeStruct, dtype=BF16)

    own_u = lax.axis_index(COL).reshape(1)
    u_blocks, keep_u, keep_v, next_rows, row_lane, col_lane, row_sub, col_sub = call(
        prepare_kernel,
        "prepare",
        [
            (cols_n, u_here, u_own),
            keep_u.T.shape,
            keep_v.T.shape,
            (v_rows, LANES),
            (1, 2 * slots),
            (1, 2 * slots),
            (2 * slots, 1),
            (2 * slots, 1),
        ],
        [
            tile_count,
            own_u,
            u_start,
            tile_rows.reshape(1, slots),
            tile_cols.reshape(1, slots),
            keep_u.T,
            keep_v.T,
            v_next.reshape(v_rows, LANES),
        ],
        scalars=(0, 1),
        scratch=[pltpu.VMEM((2, 1, slots), jnp.int32), pltpu.SemaphoreType.DMA((cols_n + 5,))],
        far=range(2, 8),
    )
    v_blocks = jnp.moveaxis(v_start.reshape(v_here, rows_n, v_own), 1, 0)
    v_got = swapped(v_blocks, ROW).reshape(-1, v_own)
    u_got = swapped(after(u_blocks, v_got), COL).reshape(-1, u_own)
    (u_kept,) = call(kept_kernel, "left_kept", [(keep, u_own)], [u_got, keep_u])
    v_got, u_later = lax.optimization_barrier((v_got, u_kept))
    u_sent = u_later.astype(jnp.float16)
    (u_gram,) = call(gram_kernel, "left_gram", [(8, LANES)], [u_later])
    u_came = turned(u_sent, COL[0], 2, 1)
    v_kept, message = call(
        kept_with_kernel,
        "right_kept",
        [(keep, v_own), (devices, 8, LANES)],
        [v_got, keep_v, next_rows],
        scratch=[pltpu.VMEM((LANES, v_own), F32)],
    )
    got, u_came = lax.optimization_barrier((swapped(message, ROW_COL), u_came))
    u_pair = jnp.stack([u_sent, u_came])
    u_pairs = [u_pair] + [turned(u_pair, COL[1], PLACES, k) for k in range(1, PLACES)]
    got = after(got, u_pair)
    v_0, gram_v, message = call(
        functools.partial(first_kernel, v_length),
        "first_right",
        [(v_rows, LANES), (PAD, LANES), (rows_n, v_rows, LANES)],
        [got, v_kept, next_rows],
    )
    tile_room = [pltpu.VMEM(tile_blocks.shape, BF16)]
    (message,) = call(
        first_forward_kernel,
        "forward",
        [narrow((cols_n, u_full + 32, LANES))],
        [swapped(message, ROW), tile_blocks, col_sub, row_lane, u_gram],
        scratch=products + sems + tile_room,
        far=(1,),
    )
    got = swapped(message, COL)
    image, dots, u_near = call(
        functools.partial(dots_kernel, u_length, True),
        "left_dots",
        [(u_full, LANES), (rows_n, 16, LANES), pltpu.VMEM((cols_n, keep, u_own), F32)],
        [own_u, got, *(pair.astype(F32) for pair in u_pairs)],
        scalars=(0,),
        scratch=sems,
        any_place=range(2, 2 + PLACES),
    )

    def left(dots, image, tiles, m, gram, others):
        known = [] if gram is None else [gram]
        keep_tiles = [] if known else tile_room
        return call(
            functools.partial(vector_kernel, m, bool(known)),
            "left",
            [(u_full, LANES), (u_rows, LANES), (PAD, LANES), (1, LANES), (rows_n, v_rows, LANES), *keep_tiles],
            [own_u, swapped(dots, ROW), image, u_near, tiles, row_sub, col_lane, *known, *others],
            scalars=(0,),
            scratch=products if known else products + sems,
            near=(3, 4) if known else (3,),
            far=() if known else (4,),
        )

    u_0_wide, u_0, gram_u, alpha_0, message, tiles = left(dots, image, tile_blocks, keep, None, [])
    image, dots = call(
        functools.partial(right_dots_kernel, v_length),
        "right_dots",
        [(v_rows, LANES), (devices, LANES)],
        [swapped(message, ROW), v_kept, v_0],
    )
    v_1, gram_v, beta_0, message = call(
        functools.partial(right_kernel, keep + 1),
        "right",
        [(v_rows, LANES), (PAD, LANES), (1, LANES), (rows_n, v_rows, LANES)],
        [swapped(dots, ROW_COL), image, v_kept, gram_v, v_0],
    )
    (message,) = call(
        forward_kernel,
        "forward",
        [narrow((cols_n, u_full, LANES))],
        [swapped(message, ROW), tiles, col_sub, row_lane],
        scratch=products,
        near=(1,),
    )
    image, dots = call(
        functools.partial(dots_kernel, u_length, False),
        "left_dots",
        [(u_full, LANES), (rows_n, LANES)],
        [own_u, swapped(message, COL), u_near, u_0_wide],
        scalars=(0,),
        near=(2,),
    )
    _, u_1, _, alpha_1, message = left(dots, image, tiles, keep + 1, gram_u, [u_0_wide])
    got = swapped(message, ROW)
    (u_basis,) = call(left_out_kernel, "left_out", [(keep + 2, u_own)], [u_kept, u_0, u_1])
    image, dots = call(
        functools.partial(right_dots_kernel, v_length),
        "last_dots",
        [(v_rows, LANES), (devices, LANES)],
        [got, v_kept, v_0, v_1],
    )
    v_basis, scales = call(
        functools.partial(last_kernel, keep + 2),
        "last_right",
        [(keep + 3, v_own), (2, 2)],
        [swapped(dots, ROW_COL), image, v_kept, gram_v, v_0, v_1, alpha_0, alpha_1, beta_0],
    )
    return u_basis, v_basis, scales


def solution(mesh):
    finer = Mesh(mesh.devices.reshape(2, 4, 2, 2, 4), ROW_COL)
    return jax.shard_map(
        per_device,
        mesh=finer,
        in_specs=(
            P(COL, ROW),
            P(ROW, COL),
            P(),
            P(),
            P(COL_ROW),
            P(ROW_COL, None, None),
            P(ROW_COL),
            P(ROW_COL),
            P(ROW_COL),
        ),
        out_specs=(P(None, ROW_COL), P(None, COL_ROW), P()),
        check_vma=False,
    )
```

```python
import functools

import jax
import jax.numpy as jnp
from jax import lax
from jax.experimental import pallas as pl
from jax.experimental.pallas import tpu as pltpu
from jax.sharding import Mesh
from jax.sharding import PartitionSpec as P

ROW = ("row_0", "row_1", "row_2")
COL = ("col_0", "col_1")
ROW_COL = ROW + COL
COL_ROW = COL + ROW

HIGH = lax.Precision.HIGHEST
F32 = jnp.float32
BF16 = jnp.bfloat16
LANES = 128
PAD = 48
PLACES = 4
EPS = 1e-06
VMEM_LIMIT = 24 << 20
CHUNKS = 8


def swapped(blocks, axis):
    return lax.all_to_all(blocks, axis, 0, 0, tiled=True)


def iota(shape, dim):
    return lax.broadcasted_iota(jnp.int32, shape, dim)


def as_row(col):
    spot = iota((PAD, LANES), 0) == iota((PAD, LANES), 1)
    return jnp.sum(jnp.where(spot, col, 0.0), axis=0, keepdims=True)


def as_col(row):
    spot = iota((PAD, LANES), 0) == iota((PAD, LANES), 1)
    return jnp.sum(jnp.where(spot, row, 0.0), axis=1, keepdims=True)


def total(x):
    return jnp.sum(jnp.sum(x, axis=1, keepdims=True), axis=0, keepdims=True)


def packed(gram, n):
    width = n // 2 + 1
    twice = gram + pltpu.roll(gram, n, 1)
    turned, sub = twice, iota((PAD, LANES), 0)
    for bit in (1, 2, 4, 8, 16, 32):
        turned = jnp.where(sub & bit != 0, pltpu.roll(turned, LANES - bit, 1), turned)
    turned = jnp.where(iota((PAD, LANES), 1) < width, turned, 0.0)
    out = turned[0:8]
    for g in range(1, PAD // 8):
        out = out + pltpu.roll(turned[8 * g : 8 * g + 8], width * g, 1)
    return out


def unpacked(pack, n):
    width = n // 2 + 1
    groups = [pack] + [
        pltpu.roll(pack, LANES - width * g, 1) for g in range(1, PAD // 8)
    ]
    turned = jnp.concatenate(groups, axis=0)
    turned = jnp.where(iota((PAD, LANES), 1) < width, turned, 0.0)
    wide = pltpu.roll(turned, 0, 1, stride=1, stride_axis=0)
    half = wide + pltpu.roll(wide, LANES - n, 1)
    lane, sub = iota((PAD, LANES), 1), iota((PAD, LANES), 0)
    half = jnp.where((lane < n) & (sub < n), half, 0.0)
    square = jnp.concatenate([half, jnp.zeros((LANES - PAD, LANES), F32)], axis=0)
    return half + jnp.where(lane == sub, 0.0, square.T[:PAD])


def solve(gram, dots_col, square, m):
    coef_col = 2.0 * dots_col - jnp.sum(gram * as_row(dots_col), axis=1, keepdims=True)
    across = dots_col - jnp.sum(gram * as_row(coef_col), axis=1, keepdims=True)
    mean_square = square - total(coef_col * (dots_col + across))
    mean_square = jnp.maximum(mean_square, 0.0)
    scale = jnp.sqrt(mean_square + EPS)
    inverse = 1.0 / scale
    across = across * inverse
    lane, sub = iota((PAD, LANES), 1), iota((PAD, LANES), 0)
    grown = jnp.where(sub == m, as_row(across), gram)
    grown = jnp.where(lane == m, across, grown)
    grown = jnp.where((lane == m) & (sub == m), mean_square * inverse * inverse, grown)
    return coef_col, scale, inverse, grown


def at(value, index):
    return jnp.where(iota((PAD, 1), 0) == index, value, 0.0)


def padded(col):
    return jnp.concatenate([col, jnp.zeros((PAD - col.shape[0], 1), F32)], axis=0)


def prepare_kernel(
    count_ref, own_ref, start_ref, rows_ref, cols_ref, keep_u_ref, keep_v_ref, next_ref,
    out_ref, keep_u_out, keep_v_out, next_out, row_lane_ref, col_lane_ref, row_sub_ref, col_sub_ref,
    index_ref, sems,
):
    blocks, _, width = out_ref.shape
    pairs = [(start_ref.at[:, k * width : (k + 1) * width], out_ref.at[k]) for k in range(blocks)]
    pairs += [(keep_u_ref, keep_u_out), (keep_v_ref, keep_v_out), (next_ref, next_out)]
    pairs += [(rows_ref, index_ref.at[0]), (cols_ref, index_ref.at[1])]
    copies = [pltpu.make_async_copy(a, b, sems.at[n]) for n, (a, b) in enumerate(pairs)]
    for copy in copies:
        copy.start()
    for copy in copies[::-1]:
        copy.wait()
    slots = rows_ref.shape[1]
    double = 2 * slots
    pair = iota((double, slots), 0) // 2 == iota((double, slots), 1)
    spot = iota((double, double), 0) == iota((double, double), 1)
    used = iota((1, double), 1) // 2 < count_ref[0]
    for n, (lane_ref, sub_ref) in enumerate(((row_lane_ref, row_sub_ref), (col_lane_ref, col_sub_ref))):
        sub = jnp.sum(jnp.where(pair, index_ref[n].astype(F32), 0.0), axis=1, keepdims=True)
        sub_ref[...] = sub
        lane = jnp.sum(jnp.where(spot, sub, 0.0), axis=0, keepdims=True)
        lane_ref[...] = jnp.where(used, lane, -1.0)


def kept_kernel(start_ref, keep_ref, out_ref):
    out_ref[...] = jnp.dot(keep_ref[...], start_ref[...], precision=HIGH, preferred_element_type=F32)


def gram_kernel(basis_ref, gram_ref):
    basis = basis_ref[...]
    rows, width = basis.shape
    wide = jnp.concatenate([basis, jnp.zeros((PAD - rows, width), F32)], axis=0)
    full = jnp.concatenate([wide, jnp.zeros((LANES - PAD, width), F32)], axis=0)
    gram = lax.dot_general(
        wide, full, (((1,), (1,)), ((), ())), precision=HIGH, preferred_element_type=F32
    )
    gram_ref[...] = packed(gram, rows + 1)


def kept_with_kernel(start_ref, keep_ref, next_ref, out_ref, message_ref, wide_ref):
    basis = jnp.dot(keep_ref[...], start_ref[...], precision=HIGH, preferred_element_type=F32)
    out_ref[...] = basis
    rows = basis.shape[0]
    wide_ref[...] = jnp.zeros_like(wide_ref)
    wide_ref[:rows] = basis
    for j in range(next_ref.shape[0]):
        wide_ref[rows : rows + 1, j * LANES : (j + 1) * LANES] = next_ref[j : j + 1]
    full = wide_ref[...]
    gram = lax.dot_general(
        full[:PAD], full, (((1,), (1,)), ((), ())), precision=HIGH, preferred_element_type=F32
    )
    message_ref[...] = jnp.broadcast_to(packed(gram, rows + 1)[None], message_ref.shape)


def projected_slice(vector_ref, basis_ref, coef_col):
    count = basis_ref.shape[0]
    rows = []
    for j in range(vector_ref.shape[0]):
        part = basis_ref[:, j * LANES : (j + 1) * LANES] * coef_col[:count]
        rows.append(jnp.sum(part, axis=0, keepdims=True))
    return vector_ref[...] - jnp.concatenate(rows, axis=0)


def first_kernel(length, got_ref, basis_ref, next_ref, vector_ref, gram_ref, message_ref):
    count = basis_ref.shape[0]
    gram = unpacked(jnp.sum(got_ref[...], axis=0), count + 1) * (1.0 / length)
    lane, sub = iota((PAD, LANES), 1), iota((PAD, LANES), 0)
    dots = jnp.sum(jnp.where((lane == count) & (sub < count), gram, 0.0), axis=1, keepdims=True)
    square = total(jnp.where((lane == count) & (sub == count), gram, 0.0))
    gram = jnp.where((lane < count) & (sub < count), gram, 0.0)
    coef, scale, inverse, grown = solve(gram, dots, square, count)
    new = projected_slice(next_ref, basis_ref, coef) * inverse
    vector_ref[...] = new
    gram_ref[...] = grown
    message_ref[...] = jnp.broadcast_to(new[None], message_ref.shape)


def started(source, target, sems):
    parts = sems.shape[0]
    step = source.shape[0] // parts
    copies = [
        pltpu.make_async_copy(
            source.at[n * step : (n + 1) * step], target.at[n * step : (n + 1) * step], sems.at[n]
        )
        for n in range(parts)
    ]
    for copy in copies:
        copy.start()
    return copies


def multiplied(forward, both, entries, tiles_ref, tile_copies, pick_ref, put_ref, picked_ref, product_ref):
    slots, size = tiles_ref.shape[:2]
    blocks = size // LANES
    rows = entries.shape[0]
    high = entries.astype(BF16)
    low = (entries - high.astype(F32)).astype(BF16)
    lane, part = iota((2 * slots, rows), 1).astype(F32), iota((2 * slots, rows), 0) % 2
    for b in range(blocks):
        spot = lane == blocks * pick_ref[...] + b
        picked = jnp.dot((spot & (part == 0)).astype(BF16), high, preferred_element_type=F32)
        if both:
            picked = picked + jnp.dot((spot & (part == 1)).astype(BF16), low, preferred_element_type=F32)
        picked_ref[:, b * LANES : (b + 1) * LANES] = picked
    for t in range(slots):
        if tile_copies and t % (slots // CHUNKS) == 0:
            tile_copies[t // (slots // CHUNKS)].wait()
        product_ref[2 * t : 2 * t + 2] = lax.dot_general(
            picked_ref[2 * t : 2 * t + 2].astype(BF16),
            tiles_ref[t],
            (((1,), (1 if forward else 0,)), ((), ())),
            preferred_element_type=F32,
        )
    sub = iota((rows, 2 * slots), 0).astype(F32)
    out = None
    for b in range(blocks):
        hot = (sub == blocks * put_ref[...] + b).astype(F32)
        part = jnp.dot(
            hot, product_ref[:, b * LANES : (b + 1) * LANES], precision=HIGH, preferred_element_type=F32
        )
        out = part if out is None else out + part
    return out


def first_forward_kernel(
    got_ref, tiles_hbm, pick_ref, put_ref, gram_ref, message_ref, picked_ref, product_ref, tile_sems, tiles_ref
):
    copies = started(tiles_hbm, tiles_ref, tile_sems)
    entries = got_ref[...].reshape(-1, LANES)
    sums = multiplied(True, False, entries, tiles_ref, copies, pick_ref, put_ref, picked_ref, product_ref).astype(BF16)
    rows = sums.shape[0]
    gram = gram_ref[...]
    high = gram.astype(BF16).astype(F32)
    middle = (gram - high).astype(BF16).astype(F32)
    low = gram - high - middle
    first = jnp.concatenate([high, middle], axis=0).astype(BF16)
    second = jnp.concatenate([low, jnp.zeros_like(low)], axis=0).astype(BF16)
    for k in range(message_ref.shape[0]):
        message_ref[k, :rows] = sums
        message_ref[k, rows : rows + 16] = first
        message_ref[k, rows + 16 : rows + 32] = second


def forward_kernel(got_ref, tiles_ref, pick_ref, put_ref, message_ref, picked_ref, product_ref):
    entries = got_ref[...].reshape(-1, LANES)
    sums = multiplied(True, True, entries, tiles_ref, [], pick_ref, put_ref, picked_ref, product_ref)
    message_ref[...] = jnp.broadcast_to(sums.astype(BF16)[None], message_ref.shape)


def dots_kernel(length, first, own_ref, got_ref, *refs):
    if first:
        *pairs, image_ref, message_ref, near_ref, sems = refs
        others = []
        ranks = [own_ref[0] ^ (PLACES * h + k) for k in range(PLACES) for h in range(2)]
        copies = [
            pltpu.make_async_copy(pairs[n // 2].at[n % 2], near_ref.at[rank], sems.at[n])
            for n, rank in enumerate(ranks)
        ]
        for copy in copies:
            copy.start()
    else:
        near_ref, *others, image_ref, message_ref = refs
        ranks, copies = range(near_ref.shape[0]), []
    image = jnp.sum(got_ref[:, :LANES].astype(F32), axis=0)
    image_ref[...] = image
    _, count, width = near_ref.shape
    across = width // LANES
    acc = jnp.zeros((count, LANES), F32)
    for n, rank in enumerate(ranks):
        if copies:
            copies[n].wait()
        start = rank * across
        part = image_ref[pl.ds(pl.multiple_of(start, across) if first else start, across)]
        for j in range(across):
            acc = acc + near_ref[rank, :, j * LANES : (j + 1) * LANES] * part[j : j + 1]
    dots = padded(jnp.sum(acc, axis=1, keepdims=True))
    for n, other in enumerate(others):
        dots = dots + at(total(other[...].reshape(image.shape) * image), count + n)
    dots = dots + at(total(image * image), PAD - 1)
    row = as_row(dots) * (1.0 / length)
    if first:
        grams = jnp.sum(got_ref[:, LANES:].astype(F32), axis=0)
        gram = (grams[:8] + grams[8:16] + grams[16:24]) * (1.0 / length)
        message_ref[:, :8] = jnp.broadcast_to(gram[None], (message_ref.shape[0], 8, LANES))
        message_ref[:, 8:] = jnp.broadcast_to(row[None], (message_ref.shape[0], 8, LANES))
    else:
        message_ref[...] = jnp.broadcast_to(row, message_ref.shape)


def split_dots(row):
    col = as_col(row)
    last = iota((PAD, 1), 0) == PAD - 1
    return jnp.where(last, 0.0, col), total(jnp.where(last, col, 0.0))


def vector_kernel(
    m, known, own_ref, got_ref, image_ref, wide_ref, tiles_ref, pick_ref, put_ref, *refs
):
    copies = []
    if known:
        *refs, picked_ref, product_ref = refs
    else:
        *refs, near_ref, picked_ref, product_ref, tile_sems = refs
        copies = started(tiles_ref, near_ref, tile_sems)
        tiles_ref = near_ref
    *inputs, new_ref, own_out_ref, gram_ref, scale_ref, message_ref = refs
    parts, count, width = wide_ref.shape
    if known:
        gram = inputs[0][...]
        row = jnp.sum(got_ref[...], axis=0, keepdims=True)
        others = inputs[1:]
    else:
        got = jnp.sum(got_ref[...], axis=0)
        gram = unpacked(got[:8], count + 1)
        row = got[8:9]
        others = inputs
    dots, square = split_dots(row)
    coef, scale, inverse, grown = solve(gram, dots, square, m)
    gram_ref[...] = grown
    scale_ref[...] = jnp.broadcast_to(scale, scale_ref.shape)
    across = width // LANES
    by_lane = jnp.broadcast_to(coef[:count], (count, LANES))
    for k in range(parts):
        sums = [
            jnp.sum(wide_ref[k, :, j * LANES : (j + 1) * LANES] * by_lane, axis=0, keepdims=True)
            for j in range(across)
        ]
        span = slice(k * across, (k + 1) * across)
        new_ref[span] = image_ref[span] - jnp.concatenate(sums, axis=0)
    new = new_ref[...]
    for n, other in enumerate(others):
        new = new - coef[count + n : count + n + 1] * other[...].reshape(new.shape)
    new = new * inverse
    new_ref[...] = new
    own_out_ref[...] = new_ref[pl.ds(pl.multiple_of(own_ref[0] * across, across), across)]
    sums = multiplied(False, True, new, tiles_ref, copies, pick_ref, put_ref, picked_ref, product_ref)
    message_ref[...] = sums.reshape(message_ref.shape)


def right_dots_kernel(length, got_ref, basis_ref, *refs):
    refs = list(refs)
    image_ref, message_ref = refs[-2:]
    others = refs[:-2]
    image = jnp.sum(got_ref[...], axis=0)
    image_ref[...] = image
    count = basis_ref.shape[0]
    acc = jnp.zeros((count, LANES), F32)
    for j in range(image.shape[0]):
        acc = acc + basis_ref[:, j * LANES : (j + 1) * LANES] * image_ref[j : j + 1]
    dots = padded(jnp.sum(acc, axis=1, keepdims=True))
    for n, other in enumerate(others):
        dots = dots + at(total(other[...] * image), count + n)
    dots = dots + at(total(image * image), PAD - 1)
    message_ref[...] = jnp.broadcast_to(as_row(dots) * (1.0 / length), message_ref.shape)


def new_right(m, got_ref, image_ref, basis_ref, gram_ref, others):
    count = basis_ref.shape[0]
    dots, square = split_dots(jnp.sum(got_ref[...], axis=0, keepdims=True))
    coef, scale, inverse, grown = solve(gram_ref[...], dots, square, m)
    new = projected_slice(image_ref, basis_ref, coef)
    for n, other in enumerate(others):
        new = new - coef[count + n : count + n + 1] * other[...]
    return new * inverse, scale, grown


def right_kernel(m, got_ref, image_ref, basis_ref, gram_in_ref, *refs):
    refs = list(refs)
    vector_ref, gram_ref, scale_ref, message_ref = refs[-4:]
    new, scale, grown = new_right(m, got_ref, image_ref, basis_ref, gram_in_ref, refs[:-4])
    vector_ref[...] = new
    gram_ref[...] = grown
    scale_ref[...] = jnp.broadcast_to(scale, scale_ref.shape)
    message_ref[...] = jnp.broadcast_to(new[None], message_ref.shape)


def put_rows(out_ref, row, vector):
    for j in range(vector.shape[0]):
        out_ref[row : row + 1, j * LANES : (j + 1) * LANES] = vector[j : j + 1]


def last_kernel(
    m, got_ref, image_ref, basis_ref, gram_ref, old_0_ref, old_1_ref,
    alpha_0_ref, alpha_1_ref, beta_0_ref, out_ref, scales_ref,
):
    new, scale, _ = new_right(m, got_ref, image_ref, basis_ref, gram_ref, [old_0_ref, old_1_ref])
    count = basis_ref.shape[0]
    out_ref[:count] = basis_ref[...]
    put_rows(out_ref, count, old_0_ref[...])
    put_rows(out_ref, count + 1, old_1_ref[...])
    put_rows(out_ref, count + 2, new)
    lane = iota((1, LANES), 1)
    alphas = jnp.where(lane == 0, alpha_0_ref[...], alpha_1_ref[...])
    betas = jnp.where(lane == 0, beta_0_ref[...], jnp.broadcast_to(scale, (1, LANES)))
    scales_ref[...] = jnp.concatenate([alphas, betas], axis=0)[:, :2]


def left_out_kernel(basis_ref, new_0_ref, new_1_ref, out_ref):
    count = basis_ref.shape[0]
    out_ref[:count] = basis_ref[...]
    put_rows(out_ref, count, new_0_ref[...])
    put_rows(out_ref, count + 1, new_1_ref[...])


WHOLE = pl.BlockSpec(memory_space=pltpu.VMEM)
SCALAR = pl.BlockSpec(memory_space=pltpu.SMEM)
ANYWHERE = pl.BlockSpec(memory_space=pl.ANY)
FAR = pl.BlockSpec(memory_space=pltpu.HBM)


def turned(x, axis, count, k):
    return lax.ppermute(x, axis, [(i, i ^ k) for i in range(count)])


def in_hbm(x):
    return pltpu.with_memory_space_constraint(x, pltpu.HBM)


def in_vmem(x):
    return pltpu.with_memory_space_constraint(x, pltpu.VMEM)


def call(kernel, name, outs, args, scalars=(), scratch=(), far=(), near=(), any_place=()):
    shapes = tuple(jax.ShapeDtypeStruct(s, F32) if isinstance(s, tuple) else s for s in outs)
    specs = [
        SCALAR if i in scalars else FAR if i in far else ANYWHERE if i in any_place else WHOLE
        for i in range(len(args))
    ]
    return pl.pallas_call(
        kernel,
        name=name,
        out_shape=shapes,
        in_specs=specs,
        out_specs=tuple(WHOLE for _ in shapes),
        scratch_shapes=list(scratch),
        compiler_params=pltpu.CompilerParams(vmem_limit_bytes=VMEM_LIMIT),
    )(*(in_hbm(x) if i in far else in_vmem(x) if i in near else x for i, x in enumerate(args)))


def after(x, *earlier):
    return lax.optimization_barrier((x, *earlier))[0]


def per_device(
    u_start, v_start, keep_u, keep_v, v_next, tile_blocks, tile_rows, tile_cols, tile_count
):
    rows_n, cols_n = lax.axis_size(ROW), lax.axis_size(COL)
    devices = rows_n * cols_n
    keep = keep_u.shape[1]
    slots, size = tile_blocks.shape[:2]
    u_here, u_range = u_start.shape
    v_here, v_range = v_start.shape
    u_own, v_own = u_range // cols_n, v_range // rows_n
    u_length, v_length = u_range * rows_n, v_range * cols_n
    u_rows, v_rows = u_own // LANES, v_own // LANES
    u_full, v_full = u_range // LANES, v_range // LANES
    products = [pltpu.VMEM((2 * slots, size), F32), pltpu.VMEM((2 * slots, size), F32)]
    sems = [pltpu.SemaphoreType.DMA((CHUNKS,))]
    narrow = functools.partial(jax.ShapeDtypeStruct, dtype=BF16)

    own_u = lax.axis_index(COL).reshape(1)
    u_blocks, keep_u, keep_v, next_rows, row_lane, col_lane, row_sub, col_sub = call(
        prepare_kernel,
        "prepare",
        [
            (cols_n, u_here, u_own),
            keep_u.T.shape,
            keep_v.T.shape,
            (v_rows, LANES),
            (1, 2 * slots),
            (1, 2 * slots),
            (2 * slots, 1),
            (2 * slots, 1),
        ],
        [
            tile_count,
            own_u,
            u_start,
            tile_rows.reshape(1, slots),
            tile_cols.reshape(1, slots),
            keep_u.T,
            keep_v.T,
            v_next.reshape(v_rows, LANES),
        ],
        scalars=(0, 1),
        scratch=[pltpu.VMEM((2, 1, slots), jnp.int32), pltpu.SemaphoreType.DMA((cols_n + 5,))],
        far=range(2, 8),
    )
    v_blocks = jnp.moveaxis(v_start.reshape(v_here, rows_n, v_own), 1, 0)
    v_got = swapped(v_blocks, ROW).reshape(-1, v_own)
    u_got = swapped(after(u_blocks, v_got), COL).reshape(-1, u_own)
    (u_kept,) = call(kept_kernel, "left_kept", [(keep, u_own)], [u_got, keep_u])
    v_kept, message = call(
        kept_with_kernel,
        "right_kept",
        [(keep, v_own), (devices, 8, LANES)],
        [v_got, keep_v, next_rows],
        scratch=[pltpu.VMEM((LANES, v_own), F32)],
    )
    message, u_later = lax.optimization_barrier((message, u_kept))
    u_sent = u_later.astype(jnp.float16)
    (u_gram,) = call(gram_kernel, "left_gram", [(8, LANES)], [u_later])
    u_came = turned(u_sent, COL[0], 2, 1)
    got, u_came = lax.optimization_barrier((swapped(message, ROW_COL), u_came))
    u_pair = jnp.stack([u_sent, u_came])
    u_pairs = [u_pair] + [turned(u_pair, COL[1], PLACES, k) for k in range(1, PLACES)]
    got = after(got, u_pair)
    v_0, gram_v, message = call(
        functools.partial(first_kernel, v_length),
        "first_right",
        [(v_rows, LANES), (PAD, LANES), (rows_n, v_rows, LANES)],
        [got, v_kept, next_rows],
    )
    tile_room = [pltpu.VMEM(tile_blocks.shape, BF16)]
    (message,) = call(
        first_forward_kernel,
        "forward",
        [narrow((cols_n, u_full + 32, LANES))],
        [swapped(message, ROW), tile_blocks, col_sub, row_lane, u_gram],
        scratch=products + sems + tile_room,
        far=(1,),
    )
    got = swapped(message, COL)
    image, dots, u_near = call(
        functools.partial(dots_kernel, u_length, True),
        "left_dots",
        [(u_full, LANES), (rows_n, 16, LANES), pltpu.VMEM((cols_n, keep, u_own), F32)],
        [own_u, got, *(pair.astype(F32) for pair in u_pairs)],
        scalars=(0,),
        scratch=sems,
        any_place=range(2, 2 + PLACES),
    )

    def left(dots, image, tiles, m, gram, others):
        known = [] if gram is None else [gram]
        keep_tiles = [] if known else tile_room
        return call(
            functools.partial(vector_kernel, m, bool(known)),
            "left",
            [(u_full, LANES), (u_rows, LANES), (PAD, LANES), (1, LANES), (rows_n, v_rows, LANES), *keep_tiles],
            [own_u, swapped(dots, ROW), image, u_near, tiles, row_sub, col_lane, *known, *others],
            scalars=(0,),
            scratch=products if known else products + sems,
            near=(3, 4) if known else (3,),
            far=() if known else (4,),
        )

    u_0_wide, u_0, gram_u, alpha_0, message, tiles = left(dots, image, tile_blocks, keep, None, [])
    image, dots = call(
        functools.partial(right_dots_kernel, v_length),
        "right_dots",
        [(v_rows, LANES), (devices, LANES)],
        [swapped(message, ROW), v_kept, v_0],
    )
    v_1, gram_v, beta_0, message = call(
        functools.partial(right_kernel, keep + 1),
        "right",
        [(v_rows, LANES), (PAD, LANES), (1, LANES), (rows_n, v_rows, LANES)],
        [swapped(dots, ROW_COL), image, v_kept, gram_v, v_0],
    )
    (message,) = call(
        forward_kernel,
        "forward",
        [narrow((cols_n, u_full, LANES))],
        [swapped(message, ROW), tiles, col_sub, row_lane],
        scratch=products,
        near=(1,),
    )
    image, dots = call(
        functools.partial(dots_kernel, u_length, False),
        "left_dots",
        [(u_full, LANES), (rows_n, LANES)],
        [own_u, swapped(message, COL), u_near, u_0_wide],
        scalars=(0,),
        near=(2,),
    )
    _, u_1, _, alpha_1, message = left(dots, image, tiles, keep + 1, gram_u, [u_0_wide])
    got = swapped(message, ROW)
    (u_basis,) = call(left_out_kernel, "left_out", [(keep + 2, u_own)], [u_kept, u_0, u_1])
    image, dots = call(
        functools.partial(right_dots_kernel, v_length),
        "last_dots",
        [(v_rows, LANES), (devices, LANES)],
        [got, v_kept, v_0, v_1],
    )
    v_basis, scales = call(
        functools.partial(last_kernel, keep + 2),
        "last_right",
        [(keep + 3, v_own), (2, 2)],
        [swapped(dots, ROW_COL), image, v_kept, gram_v, v_0, v_1, alpha_0, alpha_1, beta_0],
    )
    return u_basis, v_basis, scales


def solution(mesh):
    finer = Mesh(mesh.devices.reshape(2, 4, 2, 2, 4), ROW_COL)
    return jax.shard_map(
        per_device,
        mesh=finer,
        in_specs=(
            P(COL, ROW),
            P(ROW, COL),
            P(),
            P(),
            P(COL_ROW),
            P(ROW_COL, None, None),
            P(ROW_COL),
            P(ROW_COL),
            P(ROW_COL),
        ),
        out_specs=(P(None, ROW_COL), P(None, COL_ROW), P()),
        check_vma=False,
    )
```
